32 devices in a mesh: ctx: 8 (over z, x), head: 4 (over y, core).
Axes of the slice: x: 2, y: 2, z: 4, core: 2. Of those that a mesh axis runs over, the one named last changes fastest.
Arguments:
- queries: bfloat16 [64, 8192], P('ctx', 'head'), may hold values from -16 to 16
- keys: bfloat16 [262144, 8, 128], P('ctx', 'head'), may hold values from -16 to 16
- values: bfloat16 [262144, 8, 128], P('ctx', 'head'), may hold values from -4 to 4
- offsets: int32 [8], P('ctx'), may hold values from 0 to 229376, as said below
- lengths: int32 [64], replicated, may hold values from 131072 to 262144
- residual: bfloat16 [64, 5120], P(None, 'ctx'), may hold values from -2 to 2
- wo: bfloat16 [8192, 5120], P('head', 'ctx'), may hold values from -0.0625 to 0.0625
- norm_gain: float32 [5120], P('ctx'), may hold values from 0.1 to 1.9
- w_gate: bfloat16 [5120, 25600], P('ctx', 'head'), may hold values from -0.078125 to 0.078125
- w_up: bfloat16 [5120, 25600], P('ctx', 'head'), may hold values from -0.078125 to 0.078125
- w_down: bfloat16 [25600, 5120], P('head', 'ctx'), may hold values from -0.0390625 to 0.0390625
Outputs:
- attended: bfloat16 [64, 8192], P('ctx', 'head')
- stream: bfloat16 [64, 5120], P(None, 'ctx')
- ffn_out: bfloat16 [64, 5120], P('head', 'ctx')
The draws below stay inside these ranges and needn't reach their ends.
Inputs may be any that keep to these rules, and one draw needn't show every extreme that they name: offsets holds each of 0, 32768, ..., 229376 once.
All inputs are finite; a program needn't handle non-finite values.
Results may differ from the reference program's by a relative error of at most 0.02.
Values may be sent and summed in bfloat16 or wider, within the bound.
No kernel may reach another device: no remote copies, remote signals or barrier semaphores. Data moves between devices by JAX's collectives and lax.ppermute only.
A program may use at most 128 MiB of HBM per device.

```python
import math
import jax
import jax.numpy as jnp
from jax import lax

D = 5120
HQ = 64
KVH = 8
HD = 128
FF = 25600
B = 64
CTX_DEV = 32768
SEQ = 262144
SHARDS = 8


def shard_order(key):
    return jax.random.permutation(jax.random.fold_in(key, 31), SHARDS).astype(jnp.int32)


def draw_offsets(key, part):
    return shard_order(key) * CTX_DEV


def draw_queries(key, part):
    noise_key = jax.random.fold_in(key, 1)
    field = jax.random.normal(noise_key, (B, HQ, HD), jnp.float32)
    return jnp.clip(field, -16.0, 16.0).reshape(B, HQ * HD).astype(jnp.bfloat16)


def draw_keys(key, part):
    noise_key = jax.random.fold_in(key, 2)
    field = 2.5 * jax.random.normal(noise_key, (SEQ, KVH, HD), jnp.float32)
    return jnp.clip(field, -15.0, 15.0).astype(jnp.bfloat16)


def draw_values(key, part):
    noise_key, level_key = jax.random.split(jax.random.fold_in(key, 3))
    levels = jax.random.normal(level_key, (2 * SHARDS, KVH, HD), jnp.float32)
    levels = jnp.repeat(levels, CTX_DEV // 2, axis=0)
    noise = 0.3 * jax.random.normal(noise_key, (SEQ, KVH, HD), jnp.float32)
    return jnp.clip(noise + 0.6 * levels, -4.0, 4.0).astype(jnp.bfloat16)


def draw_residual(key, part):
    column_key, row_key, noise_key = jax.random.split(jax.random.fold_in(key, 5), 3)
    ramp = jnp.exp(jnp.linspace(0.0, math.log(3.0), D)) / math.sqrt(3.0)
    columns = ramp * 10.0 ** jax.random.uniform(column_key, (D,), jnp.float32, -0.5, 0.5)
    rows = 10.0 ** jax.random.uniform(row_key, (B, 1), jnp.float32, -0.5, 0.5)
    noise = jax.random.normal(noise_key, (B, D), jnp.float32)
    return jnp.clip(0.15 * rows * columns * noise, -2.0, 2.0).astype(jnp.bfloat16)


def place_ends(values, own_key, smallest, top_value):
    longest = values.shape.index(max(values.shape))
    spots = []
    for shift in (0, 1):
        where = [jax.random.randint(jax.random.fold_in(own_key, axis), (), 0, length) for axis, length in enumerate(values.shape)]
        where[longest] = (where[longest] + shift) % values.shape[longest]
        spots.append(tuple(where))
    return values.at[spots[0]].set(smallest).at[spots[1]].set(top_value)


def shard_levels(stream_key, shape, cuts, low, high):
    def one(axis_at, parts):
        steps = jax.random.uniform(jax.random.fold_in(jax.random.fold_in(stream_key, 6), axis_at), (parts,), jnp.float32, low / len(cuts), high / len(cuts))
        return jnp.repeat(jnp.exp(steps), shape[axis_at] // parts).reshape((-1,) + (1,) * (len(shape) - axis_at - 1))

    level = one(*cuts[0])
    for cut in cuts[1:]:
        level = level * one(*cut)
    return level


def normal_values(key, extent, width, most, pieces=(), kind=jnp.bfloat16):
    values = jax.random.normal(key, extent, jnp.float32) * width
    if len(pieces) > 0:
        values = shard_levels(key, extent, pieces, -0.22, 0.18) * values
    return jnp.clip(values, min=-most, max=most).astype(kind)


def setup_inputs(seed: int = 0) -> dict:
    streams_of = jax.random.split(jax.random.key(seed), 12)
    queries = draw_queries(jax.random.fold_in(streams_of[11], 71), 0)
    keys = draw_keys(jax.random.fold_in(streams_of[11], 71), 0)
    values = draw_values(jax.random.fold_in(streams_of[11], 71), 0)
    offsets = draw_offsets(jax.random.fold_in(streams_of[11], 71), 0)
    lengths = place_ends(jax.random.randint(streams_of[4], (B,), SEQ // 2, SEQ + 1), jax.random.fold_in(streams_of[4], 1), SEQ // 2, SEQ).astype(jnp.int32)
    residual = draw_residual(jax.random.fold_in(streams_of[11], 71), 0)
    wo = normal_values(streams_of[6], (HQ * HD, D), (HQ * HD) ** -0.5, 0.0625, ((0, 4), (1, 8)))
    norm_gain = jnp.clip(1.0 + 0.18 * jax.random.normal(streams_of[7], (D,), jnp.float32), 0.1, 1.9)
    w_gate = normal_values(streams_of[8], (D, FF), D ** -0.5, 0.078125, ((0, 8), (1, 4)))
    w_up = normal_values(streams_of[9], (D, FF), D ** -0.5, 0.078125, ((0, 8), (1, 4)))
    w_down = normal_values(streams_of[10], (FF, D), FF ** -0.5, 0.0390625, ((0, 4), (1, 8)))
    return {"queries": queries, "keys": keys, "values": values, "offsets": offsets, "lengths": lengths, "residual": residual, "wo": wo, "norm_gain": norm_gain, "w_gate": w_gate, "w_up": w_up, "w_down": w_down}


masked_score = -1e+30
epsilon = 1e-06

def reference(queries, keys, values, offsets, lengths, residual, wo, norm_gain, w_gate, w_up, w_down):
    groups = HQ // KVH
    query_heads = queries.astype(jnp.float32).reshape(B, KVH, groups, HD)
    query_heads = query_heads.transpose(1, 0, 2, 3).reshape(KVH, B * groups, HD)
    row_limit = jnp.repeat(lengths, groups)
    inverse_root = 1.0 / math.sqrt(HD)

    def visit(carry, shard_index):
        row_high, row_total, row_acc = carry
        first_slot = (shard_index * CTX_DEV).astype(jnp.int32)
        key_block = lax.dynamic_slice_in_dim(keys, first_slot, CTX_DEV, 0).astype(jnp.float32)
        value_block = lax.dynamic_slice_in_dim(values, first_slot, CTX_DEV, 0).astype(jnp.float32)
        scores = jnp.einsum('hrd,khd->hrk', query_heads, key_block) * inverse_root
        position = offsets[shard_index] + jnp.arange(CTX_DEV, dtype=jnp.int32)
        scores = jnp.where(position[None, None, :] < row_limit[None, :, None], scores, masked_score)
        new_high = jnp.maximum(row_high, lax.optimization_barrier(jnp.max(scores, axis=2)))
        weights = jnp.exp(scores - new_high[:, :, None])
        rounded = lax.optimization_barrier(weights.astype(jnp.bfloat16)).astype(jnp.float32)
        rescale = jnp.exp(row_high - new_high)
        row_total = row_total * rescale + lax.optimization_barrier(jnp.sum(weights, axis=2))
        row_acc = row_acc * rescale[:, :, None] + jnp.einsum('hrk,khd->hrd', rounded, value_block)
        return ((new_high, row_total, row_acc), None)
    start_high = jnp.full((KVH, B * groups), masked_score, jnp.float32)
    start_total = jnp.zeros((KVH, B * groups), jnp.float32)
    start_acc = jnp.zeros((KVH, B * groups, HD), jnp.float32)
    (row_high, row_total, row_acc), _ = lax.scan(visit, (start_high, start_total, start_acc), jnp.arange(SHARDS, dtype=jnp.int32))
    merged = row_acc / row_total[:, :, None]
    merged = merged.reshape(KVH, B, groups, HD).transpose(1, 0, 2, 3).reshape(B, HQ * HD)
    attended = merged.astype(jnp.bfloat16)
    projected = jnp.dot(attended, wo, preferred_element_type=jnp.float32)
    combined = residual.astype(jnp.float32) + projected
    stream = combined.astype(jnp.bfloat16)
    scale = lax.rsqrt(lax.optimization_barrier(jnp.sum(combined * combined, axis=1)) / D + epsilon)[:, None]
    normed = (combined * norm_gain).astype(jnp.bfloat16)
    gate = scale * jnp.dot(normed, w_gate, preferred_element_type=jnp.float32)
    upward = scale * jnp.dot(normed, w_up, preferred_element_type=jnp.float32)
    hidden = (jax.nn.silu(gate) * upward).astype(jnp.bfloat16)
    ffn_out = jnp.dot(hidden, w_down, preferred_element_type=jnp.float32).astype(jnp.bfloat16)
    return (attended, stream, ffn_out)
```

```python
import functools
import math

import jax
import jax.numpy as jnp
from jax import lax
from jax.experimental import pallas as pl
from jax.experimental.pallas import tpu as pltpu
from jax.sharding import PartitionSpec as P

hidden_score = -1e30
lowest_base = -65536.0
largest_sum = 2.0**115
epsilon = 1e-06
lane = 128


def split_heads(block, kv_local, head_size):
    flat = block.reshape(block.shape[0], kv_local * head_size)
    return [flat[:, h * head_size : (h + 1) * head_size] for h in range(kv_local)]


def hidden_slots(first_slot, count, limits):
    slot = lax.broadcasted_iota(jnp.int32, (count, limits.shape[1]), 0) + first_slot
    return jnp.where(slot < limits, 0.0, 1.0).astype(jnp.bfloat16)


def scores_of(key_block, hidden, query_cols):
    return jnp.dot(
        jnp.concatenate([key_block, hidden], axis=1), query_cols, preferred_element_type=jnp.float32
    )


def weighted_values(value_block, weights):
    return lax.dot_general(
        value_block,
        weights.astype(jnp.bfloat16),
        (((0,), (0,)), ((), ())),
        preferred_element_type=jnp.float32,
    )


def sublane_sums(weights):
    return jnp.sum(weights.reshape(weights.shape[0] // 8, 8, weights.shape[1]), axis=0)


def attention_kernel(
    query_ref,
    limit_ref,
    key_ref,
    value_ref,
    all_keys,
    all_values,
    out_ref,
    query_cols,
    base_ref,
    acc_ref,
    total_ref,
    spare_keys,
    spare_values,
    copy_sems,
    *,
    kv_local,
    groups,
    sources,
    factor,
):
    step = pl.program_id(0)
    batch = query_ref.shape[0]
    head_size = key_ref.shape[2]
    block = key_ref.shape[0]
    columns = batch * groups
    extra = limit_ref.shape[1]
    limits = limit_ref[...]

    @pl.when(step == 0)
    def start():
        row = lax.broadcasted_iota(jnp.int32, (extra, columns), 0)
        column = lax.broadcasted_iota(jnp.int32, (extra, columns), 1)
        mask_rows = jnp.where(lax.rem(column, batch) == row, hidden_score, 0.0)
        probe = min(512, block)
        hidden = hidden_slots(0, probe, limits)
        first_keys = split_heads(key_ref[pl.ds(0, probe)], kv_local, head_size)
        for h in range(kv_local):
            rows = [
                query_ref[:, (h * groups + g) * head_size : (h * groups + g + 1) * head_size]
                for g in range(groups)
            ]
            turned = jnp.concatenate(rows, axis=0).astype(jnp.float32).T
            query_cols[h, :head_size] = turned.astype(jnp.bfloat16)
            query_cols[h, head_size:] = mask_rows.astype(jnp.bfloat16)
            top = jnp.max(
                scores_of(first_keys[h], hidden, query_cols[h]), axis=0, keepdims=True
            )
            base = jnp.maximum(top, lowest_base).astype(jnp.bfloat16).astype(jnp.float32)
            base_ref[h] = base
            query_cols[h, head_size:] = jnp.where(row == batch, -base, mask_rows).astype(
                jnp.bfloat16
            )
        acc_ref[...] = jnp.zeros_like(acc_ref)
        total_ref[...] = jnp.zeros_like(total_ref)

    hidden = hidden_slots(step * block, block, limits)
    keys = split_heads(key_ref[...], kv_local, head_size)
    values = split_heads(value_ref[...], kv_local, head_size)
    for h in range(kv_local):
        weights = jnp.exp2(scores_of(keys[h], hidden, query_cols[h]) * factor)
        total_ref[h] += sublane_sums(weights)
        acc_ref[h] += weighted_values(values[h], weights)

    @pl.when(step == pl.num_programs(0) - 1)
    def finish():
        @pl.when(jnp.logical_not(jnp.max(total_ref[...]) <= largest_sum))
        def redo():
            piece = spare_keys.shape[0]
            for h in range(kv_local):
                row = lax.broadcasted_iota(jnp.int32, (extra, columns), 0)
                old = query_cols[h, head_size:].astype(jnp.float32)
                query_cols[h, head_size:] = jnp.where(row == batch, 0.0, old).astype(jnp.bfloat16)
            base_ref[...] = jnp.full_like(base_ref, lowest_base)
            acc_ref[...] = jnp.zeros_like(acc_ref)
            total_ref[...] = jnp.zeros_like(total_ref)

            def visit(turn, carry):
                first = turn * piece
                here = pl.ds(first, piece)
                get_keys = pltpu.make_async_copy(all_keys.at[here], spare_keys, copy_sems.at[0])
                get_values = pltpu.make_async_copy(
                    all_values.at[here], spare_values, copy_sems.at[1]
                )
                get_keys.start()
                get_values.start()
                get_keys.wait()
                get_values.wait()
                hidden = hidden_slots(first, piece, limits)
                keys = split_heads(spare_keys[...], kv_local, head_size)
                values = split_heads(spare_values[...], kv_local, head_size)
                for h in range(kv_local):
                    scores = scores_of(keys[h], hidden, query_cols[h])
                    old = base_ref[h]
                    new = jnp.maximum(old, jnp.max(scores, axis=0, keepdims=True))
                    rescale = jnp.exp2((old - new) * factor)
                    weights = jnp.exp2((scores - new) * factor)
                    base_ref[h] = new
                    total_ref[h] = total_ref[h] * rescale + sublane_sums(weights)
                    acc_ref[h] = acc_ref[h] * rescale + weighted_values(values[h], weights)
                return carry

            lax.fori_loop(0, all_keys.shape[0] // piece, visit, 0)

        rows_local = batch // sources
        stat_row = lax.broadcasted_iota(jnp.int32, (head_size, columns), 0)
        stats = jnp.zeros((head_size, columns), jnp.float32)
        for h in range(kv_local):
            total = jnp.sum(total_ref[h], axis=0, keepdims=True)
            seen = total > 0.0
            safe = jnp.where(seen, total, 1.0)
            height = jnp.where(seen, base_ref[h] * factor + jnp.log2(safe), hidden_score)
            for piece in range(3):
                part = height.astype(jnp.bfloat16).astype(jnp.float32)
                stats = jnp.where(stat_row == 3 * h + piece, part, stats)
                height = height - part
            mean = (acc_ref[h] * (1.0 / safe)).T.astype(jnp.bfloat16)
            for c in range(sources):
                for g in range(groups):
                    out_ref[c, h, g * rows_local : (g + 1) * rows_local] = mean[
                        g * batch + c * rows_local : g * batch + (c + 1) * rows_local
                    ]
        stats = stats.T.astype(jnp.bfloat16)
        for c in range(sources):
            for g in range(groups):
                out_ref[c, kv_local, g * rows_local : (g + 1) * rows_local] = stats[
                    g * batch + c * rows_local : g * batch + (c + 1) * rows_local
                ]


def attention(queries, limits, keys, values, sources, groups):
    span, kv_local, head_size = keys.shape
    batch = queries.shape[0]
    columns = batch * groups
    block = math.gcd(4096, span)
    piece = math.gcd(1024, span)
    extra = limits.shape[1]
    whole = lambda *shape: pl.BlockSpec(shape, lambda j: (0,) * len(shape))
    part = pl.BlockSpec((block, kv_local, head_size), lambda j: (j, 0, 0))
    out = (sources, kv_local + 1, columns // sources, head_size)
    return pl.pallas_call(
        functools.partial(
            attention_kernel,
            kv_local=kv_local,
            groups=groups,
            sources=sources,
            factor=math.log2(math.e) / math.sqrt(head_size),
        ),
        grid=(span // block,),
        in_specs=[
            whole(batch, queries.shape[1]),
            whole(1, extra),
            part,
            part,
            pl.BlockSpec(memory_space=pl.ANY),
            pl.BlockSpec(memory_space=pl.ANY),
        ],
        out_specs=whole(*out),
        out_shape=jax.ShapeDtypeStruct(out, jnp.bfloat16),
        scratch_shapes=[
            pltpu.VMEM((kv_local, head_size + extra, columns), jnp.bfloat16),
            pltpu.VMEM((kv_local, 1, columns), jnp.float32),
            pltpu.VMEM((kv_local, head_size, columns), jnp.float32),
            pltpu.VMEM((kv_local, 8, columns), jnp.float32),
            pltpu.VMEM((piece, kv_local, head_size), jnp.bfloat16),
            pltpu.VMEM((piece, kv_local, head_size), jnp.bfloat16),
            pltpu.SemaphoreType.DMA((2,)),
        ],
        compiler_params=pltpu.CompilerParams(
            dimension_semantics=("arbitrary",), vmem_limit_bytes=48 * 2**20
        ),
        cost_estimate=pl.CostEstimate(
            flops=4 * span * columns * kv_local * head_size,
            bytes_accessed=4 * span * kv_local * head_size,
            transcendentals=span * columns * kv_local,
        ),
    )(queries, limits, keys, values, keys, values)


def merge_kernel(part_ref, out_ref, *, kv_local, groups):
    sources, _, rows, head_size = part_ref.shape
    rows_local = rows // groups
    for h in range(kv_local):
        heights = []
        for c in range(sources):
            stats = part_ref[c, kv_local].astype(jnp.float32)
            heights.append(
                stats[:, 3 * h : 3 * h + 1]
                + stats[:, 3 * h + 1 : 3 * h + 2]
                + stats[:, 3 * h + 2 : 3 * h + 3]
            )
        top = functools.reduce(jnp.maximum, heights)
        shares = [jnp.exp2(height - top) for height in heights]
        whole = sum(shares)
        mean = sum(
            share * part_ref[c, h].astype(jnp.float32) for c, share in enumerate(shares)
        ) / whole
        for g in range(groups):
            out_ref[:, (h * groups + g) * head_size : (h * groups + g + 1) * head_size] = mean[
                g * rows_local : (g + 1) * rows_local
            ].astype(jnp.bfloat16)


def merge(parts, kv_local, groups):
    rows_local = parts.shape[2] // groups
    return pl.pallas_call(
        functools.partial(merge_kernel, kv_local=kv_local, groups=groups),
        out_shape=jax.ShapeDtypeStruct(
            (rows_local, kv_local * groups * parts.shape[3]), jnp.bfloat16
        ),
    )(parts)


def gather_rows(block, sources):
    copies = jnp.broadcast_to(block[None], (sources,) + block.shape)
    gathered = lax.all_to_all(copies, "ctx", split_axis=0, concat_axis=0)
    return gathered.reshape((sources * block.shape[0],) + block.shape[1:])


def swap(block, axis, size, bit):
    return lax.ppermute(block, axis, [(i, i ^ bit) for i in range(size)])


def sum_over_head(block, size):
    bit = 1
    while bit < size:
        block = block + swap(block, "head", size, bit)
        bit *= 2
    return block


def scatter_sum_over_head(block, size):
    me = lax.axis_index("head")
    bit = size // 2
    while bit >= 1:
        halves = block.reshape((2, block.shape[0] // 2) + block.shape[1:])
        side = lax.rem(me // bit, 2)
        keep = lax.dynamic_index_in_dim(halves, side, 0, keepdims=False)
        give = lax.dynamic_index_in_dim(halves, 1 - side, 0, keepdims=False)
        block = keep + swap(give, "head", size, bit)
        bit //= 2
    return block


def three_parts(column):
    parts = []
    for _ in range(3):
        part = column.astype(jnp.bfloat16)
        parts.append(part)
        column = column - part.astype(jnp.float32)
    return jnp.stack(parts, axis=-1)


def local_step(sources, heads):
    def local(
        queries, keys, values, offsets, lengths, residual, wo, norm_gain, w_gate, w_up, w_down
    ):
        head_size = keys.shape[2]
        kv_local = keys.shape[1]
        rows_local = queries.shape[0]
        groups = queries.shape[1] // (kv_local * head_size)
        batch = lengths.shape[0]
        width = residual.shape[1] * sources
        everyone = gather_rows(queries, sources)
        extra = -(-(batch + 1) // lane) * lane
        limits = jnp.full((extra,), jnp.iinfo(jnp.int32).max, jnp.int32)
        limits = limits.at[:batch].set(lengths - offsets[0]).at[batch].set(-1)
        parts = attention(everyone, limits[None], keys, values, sources, groups)
        parts = lax.all_to_all(parts, "ctx", split_axis=0, concat_axis=0)
        attended = merge(parts, kv_local, groups)
        projected = jnp.dot(
            gather_rows(attended, sources), wo, preferred_element_type=jnp.float32
        )
        combined = residual.astype(jnp.float32) + sum_over_head(projected, heads)
        stream = combined.astype(jnp.bfloat16)
        squares = three_parts(jnp.sum(combined * combined, axis=1))
        normed = (combined * norm_gain).astype(jnp.bfloat16)
        gate_part = jnp.dot(normed, w_gate, preferred_element_type=jnp.float32)
        up_part = jnp.dot(normed, w_up, preferred_element_type=jnp.float32)
        hidden_units = w_gate.shape[1]
        terms = jnp.concatenate(
            [
                gate_part.astype(jnp.bfloat16),
                up_part.astype(jnp.bfloat16),
                jnp.pad(squares, ((0, 0), (0, lane - squares.shape[1]))),
            ],
            axis=1,
        )
        terms = lax.all_to_all(
            terms.reshape(sources, rows_local, -1), "ctx", split_axis=0, concat_axis=0
        )
        terms = jnp.sum(terms.astype(jnp.float32), axis=0)
        square_total = jnp.sum(terms[:, 2 * hidden_units : 2 * hidden_units + 3], axis=1)
        scale = lax.rsqrt(square_total / width + epsilon)[:, None]
        gate = scale * terms[:, :hidden_units]
        upward = scale * terms[:, hidden_units : 2 * hidden_units]
        hidden = (jax.nn.silu(gate) * upward).astype(jnp.bfloat16)
        down = jnp.dot(
            gather_rows(hidden, sources), w_down, preferred_element_type=jnp.float32
        )
        ffn_out = scatter_sum_over_head(down, heads).astype(jnp.bfloat16)
        return (attended, stream, ffn_out)

    return local


def solution(mesh):
    return jax.shard_map(
        local_step(mesh.shape["ctx"], mesh.shape["head"]),
        mesh=mesh,
        in_specs=(
            P("ctx", "head"),
            P("ctx", "head", None),
            P("ctx", "head", None),
            P("ctx"),
            P(),
            P(None, "ctx"),
            P("head", "ctx"),
            P("ctx"),
            P("ctx", "head"),
            P("ctx", "head"),
            P("head", "ctx"),
        ),
        out_specs=(P("ctx", "head"), P(None, "ctx"), P("head", "ctx")),
        check_vma=False,
    )
```

```python
import functools
import math

import jax
import jax.numpy as jnp
from jax import lax
from jax.experimental import pallas as pl
from jax.experimental.pallas import tpu as pltpu
from jax.sharding import PartitionSpec as P

hidden_score = -1e30
lowest_base = -65536.0
largest_sum = 2.0**115
epsilon = 1e-06
lane = 128
stat_rows = 16
attention_vmem = 32 * 2**20
most_vmem = 56 * 2**20
small_vmem = 8 * 2**20


def split_heads(block, kv_local, head_size):
    flat = block.reshape(block.shape[0], kv_local * head_size)
    return [flat[:, h * head_size : (h + 1) * head_size] for h in range(kv_local)]


def hidden_slots(first_slot, count, limits):
    slot = lax.broadcasted_iota(jnp.int32, (count, limits.shape[1]), 0) + first_slot
    return jnp.where(slot < limits, 0.0, 1.0).astype(jnp.bfloat16)


def scores_of(key_block, hidden, query_cols):
    return jnp.dot(
        jnp.concatenate([key_block, hidden], axis=1), query_cols, preferred_element_type=jnp.float32
    )


def weighted_values(value_block, weights):
    return lax.dot_general(
        value_block,
        weights.astype(jnp.bfloat16),
        (((0,), (0,)), ((), ())),
        preferred_element_type=jnp.float32,
    )


def sublane_sums(weights):
    return jnp.sum(weights.reshape(weights.shape[0] // 8, 8, weights.shape[1]), axis=0)


def query_kernel(query_ref, limit_ref, key_ref, cols_ref, base_ref, *, kv_local, groups):
    batch = query_ref.shape[0]
    head_size = key_ref.shape[2]
    columns = batch * groups
    extra = limit_ref.shape[1]
    row = lax.broadcasted_iota(jnp.int32, (extra, columns), 0)
    column = lax.broadcasted_iota(jnp.int32, (extra, columns), 1)
    mask_rows = jnp.where(lax.rem(column, batch) == row, hidden_score, 0.0)
    hidden = hidden_slots(0, key_ref.shape[0], limit_ref[...])
    keys = split_heads(key_ref[...], kv_local, head_size)
    for h in range(kv_local):
        rows = [
            query_ref[:, (h * groups + g) * head_size : (h * groups + g + 1) * head_size]
            for g in range(groups)
        ]
        turned = jnp.concatenate(rows, axis=0).astype(jnp.float32).T
        cols_ref[h, :head_size] = turned.astype(jnp.bfloat16)
        cols_ref[h, head_size:] = mask_rows.astype(jnp.bfloat16)
        top = jnp.max(scores_of(keys[h], hidden, cols_ref[h]), axis=0, keepdims=True)
        base = jnp.maximum(top, lowest_base).astype(jnp.bfloat16).astype(jnp.float32)
        base_ref[h] = base
        cols_ref[h, head_size:] = jnp.where(row == batch, -base, mask_rows).astype(jnp.bfloat16)


def attention_kernel(
    query_cols,
    first_base,
    limit_ref,
    key_ref,
    value_ref,
    all_keys,
    all_values,
    *rest,
    kv_local,
    groups,
    sources,
    factor,
    carried,
):
    weights_in, rest = rest[:carried], rest[carried:]
    out_ref, weights_out, rest = rest[0], rest[1 : 1 + carried], rest[1 + carried :]
    (
    base_ref,
    acc_ref,
    total_ref,
    plain_cols,
    spare_keys,
    spare_values,
    copy_sems,
    weight_sems,
    ) = rest
    step = pl.program_id(0)
    head_size = key_ref.shape[2]
    block = key_ref.shape[0]
    columns = query_cols.shape[2]
    batch = columns // groups
    extra = limit_ref.shape[1]
    limits = limit_ref[...]
    steps = all_keys.shape[0] // block

    turns = [
        max(t for t in range(1, steps + 1) if weight.shape[0] % (16 * t) == 0)
        for weight in weights_in
    ]

    def weight_copies(index, turn):
        rows = weights_in[index].shape[0] // turns[index]
        here = pl.ds(pl.multiple_of(turn * rows, 16), rows)
        return pltpu.make_async_copy(
            weights_in[index].at[here], weights_out[index].at[here], weight_sems.at[index, turn]
        )

    for index in range(carried):
        pl.when(step < turns[index])(weight_copies(index, step).start)

    @pl.when(step == 0)
    def start():
        base_ref[...] = first_base[...]
        acc_ref[...] = jnp.zeros_like(acc_ref)
        total_ref[...] = jnp.zeros_like(total_ref)

    hidden = hidden_slots(step * block, block, limits)
    keys = split_heads(key_ref[...], kv_local, head_size)
    values = split_heads(value_ref[...], kv_local, head_size)
    for h in range(kv_local):
        weights = jnp.exp2(scores_of(keys[h], hidden, query_cols[h]) * factor)
        total_ref[h] += sublane_sums(weights)
        acc_ref[h] += weighted_values(values[h], weights)

    @pl.when(step == pl.num_programs(0) - 1)
    def finish():
        @pl.when(jnp.logical_not(jnp.max(total_ref[...]) <= largest_sum))
        def redo():
            piece = spare_keys.shape[0]
            row = lax.broadcasted_iota(jnp.int32, (head_size + extra, columns), 0)
            for h in range(kv_local):
                old = query_cols[h].astype(jnp.float32)
                plain_cols[h] = jnp.where(row == head_size + batch, 0.0, old).astype(jnp.bfloat16)
            base_ref[...] = jnp.full_like(base_ref, lowest_base)
            acc_ref[...] = jnp.zeros_like(acc_ref)
            total_ref[...] = jnp.zeros_like(total_ref)

            def visit(turn, carry):
                first = turn * piece
                here = pl.ds(first, piece)
                get_keys = pltpu.make_async_copy(all_keys.at[here], spare_keys, copy_sems.at[0])
                get_values = pltpu.make_async_copy(
                    all_values.at[here], spare_values, copy_sems.at[1]
                )
                get_keys.start()
                get_values.start()
                get_keys.wait()
                get_values.wait()
                hidden = hidden_slots(first, piece, limits)
                keys = split_heads(spare_keys[...], kv_local, head_size)
                values = split_heads(spare_values[...], kv_local, head_size)
                for h in range(kv_local):
                    scores = scores_of(keys[h], hidden, plain_cols[h])
                    old = base_ref[h]
                    new = jnp.maximum(old, jnp.max(scores, axis=0, keepdims=True))
                    rescale = jnp.exp2((old - new) * factor)
                    weights = jnp.exp2((scores - new) * factor)
                    base_ref[h] = new
                    total_ref[h] = total_ref[h] * rescale + sublane_sums(weights)
                    acc_ref[h] = acc_ref[h] * rescale + weighted_values(values[h], weights)
                return carry

            lax.fori_loop(0, all_keys.shape[0] // piece, visit, 0)

        for index in range(carried):
            for turn in range(turns[index]):
                weight_copies(index, turn).wait()
        rows_local = batch // sources
        rows = groups * rows_local
        stats = jnp.zeros((stat_rows, columns), jnp.float32)
        stat_row = lax.broadcasted_iota(jnp.int32, (stat_rows, columns), 0)
        for h in range(kv_local):
            total = jnp.sum(total_ref[h], axis=0, keepdims=True)
            seen = total > 0.0
            safe = jnp.where(seen, total, 1.0)
            height = jnp.where(seen, base_ref[h] * factor + jnp.log2(safe), hidden_score)
            for piece in range(3):
                part = height.astype(jnp.bfloat16).astype(jnp.float32)
                stats = jnp.where(stat_row == 3 * h + piece, part, stats)
                height = height - part
            mean = (acc_ref[h] * (1.0 / safe)).T.astype(jnp.bfloat16)
            for c in range(sources):
                for g in range(groups):
                    out_ref[c, h * rows + g * rows_local : h * rows + (g + 1) * rows_local] = mean[
                        g * batch + c * rows_local : g * batch + (c + 1) * rows_local
                    ]
        here = lax.broadcasted_iota(jnp.int32, (columns, columns), 0)
        there = lax.broadcasted_iota(jnp.int32, (columns, columns), 1)
        source, place = lax.div(there, rows), lax.rem(there, rows)
        origin = lax.div(place, rows_local) * batch + source * rows_local + lax.rem(place, rows_local)
        stats = jnp.dot(
            stats.astype(jnp.bfloat16),
            jnp.where(here == origin, 1.0, 0.0).astype(jnp.bfloat16),
            preferred_element_type=jnp.float32,
        )
        for c in range(sources):
            out_ref[c, kv_local * rows :, :rows] = stats[:, c * rows : (c + 1) * rows].astype(
                jnp.bfloat16
            )


def attention(queries, limits, keys, values, sources, groups, weights=()):
    span, kv_local, head_size = keys.shape
    batch = queries.shape[0]
    columns = batch * groups
    block = math.gcd(4096, span)
    piece = math.gcd(1024, span)
    extra = limits.shape[1]
    whole = lambda *shape: pl.BlockSpec(shape, lambda j: (0,) * len(shape))
    part = pl.BlockSpec((block, kv_local, head_size), lambda j: (j, 0, 0))
    out = (sources, kv_local * columns // sources + stat_rows, head_size)
    depth = head_size + extra
    probe = math.gcd(512, span)
    query_cols, base = pl.pallas_call(
        functools.partial(query_kernel, kv_local=kv_local, groups=groups),
        grid=(1,),
        in_specs=[
            whole(batch, queries.shape[1]),
            whole(1, extra),
            pl.BlockSpec((probe, kv_local, head_size), lambda j: (0, 0, 0)),
        ],
        out_specs=[whole(kv_local, depth, columns), whole(kv_local, 1, columns)],
        out_shape=[
            jax.ShapeDtypeStruct((kv_local, depth, columns), jnp.bfloat16),
            jax.ShapeDtypeStruct((kv_local, 1, columns), jnp.float32),
        ],
        compiler_params=pltpu.CompilerParams(vmem_limit_bytes=most_vmem),
    )(queries, limits, keys)
    return pl.pallas_call(
        functools.partial(
            attention_kernel,
            kv_local=kv_local,
            groups=groups,
            sources=sources,
            factor=math.log2(math.e) / math.sqrt(head_size),
            carried=len(weights),
        ),
        grid=(span // block,),
        in_specs=[
            whole(kv_local, depth, columns),
            whole(kv_local, 1, columns),
            whole(1, extra),
            part,
            part,
            pl.BlockSpec(memory_space=pl.ANY),
            pl.BlockSpec(memory_space=pl.ANY),
        ]
        + [pl.BlockSpec(memory_space=pl.ANY)] * len(weights),
        out_specs=[whole(*out)] + [pl.BlockSpec(memory_space=pltpu.VMEM)] * len(weights),
        out_shape=[jax.ShapeDtypeStruct(out, jnp.bfloat16)]
        + [pltpu.VMEM(weight.shape, weight.dtype) for weight in weights],
        scratch_shapes=[
            pltpu.VMEM((kv_local, 1, columns), jnp.float32),
            pltpu.VMEM((kv_local, head_size, columns), jnp.float32),
            pltpu.VMEM((kv_local, 8, columns), jnp.float32),
            pltpu.VMEM((kv_local, head_size + extra, columns), jnp.bfloat16),
            pltpu.VMEM((piece, kv_local, head_size), jnp.bfloat16),
            pltpu.VMEM((piece, kv_local, head_size), jnp.bfloat16),
            pltpu.SemaphoreType.DMA((2,)),
            pltpu.SemaphoreType.DMA((len(weights), span // block)),
        ],
        compiler_params=pltpu.CompilerParams(
            dimension_semantics=("arbitrary",), vmem_limit_bytes=attention_vmem
        ),
        cost_estimate=pl.CostEstimate(
            flops=4 * span * columns * kv_local * head_size,
            bytes_accessed=4 * span * kv_local * head_size,
            transcendentals=span * columns * kv_local,
        ),
    )(query_cols, base, limits, keys, values, keys, values, *weights)


def merge_kernel(part_ref, out_ref, copies_ref, *, kv_local, groups):
    sources, depth, head_size = part_ref.shape
    rows = (depth - stat_rows) // kv_local
    rows_local = rows // groups
    stats = part_ref[:, kv_local * rows :].astype(jnp.float32)
    stats = stats.reshape(sources * stat_rows, head_size).T
    for h in range(kv_local):
        heights = []
        for c in range(sources):
            first = c * stat_rows + 3 * h
            heights.append(
                stats[:rows, first : first + 1]
                + stats[:rows, first + 1 : first + 2]
                + stats[:rows, first + 2 : first + 3]
            )
        top = functools.reduce(jnp.maximum, heights)
        shares = [jnp.exp2(height - top) for height in heights]
        whole = sum(shares)
        mean = (
            sum(
                share * part_ref[c, h * rows : (h + 1) * rows].astype(jnp.float32)
                for c, share in enumerate(shares)
            )
            / whole
        )
        for g in range(groups):
            out_ref[:, (h * groups + g) * head_size : (h * groups + g + 1) * head_size] = mean[
                g * rows_local : (g + 1) * rows_local
            ].astype(jnp.bfloat16)
    copies_ref[...] = jnp.broadcast_to(out_ref[...][None], copies_ref.shape)


def merge(parts, kv_local, groups):
    sources, depth, head_size = parts.shape
    rows_local = (depth - stat_rows) // kv_local // groups
    width = kv_local * groups * head_size
    return pl.pallas_call(
        functools.partial(merge_kernel, kv_local=kv_local, groups=groups),
        out_shape=[
            jax.ShapeDtypeStruct((rows_local, width), jnp.bfloat16),
            jax.ShapeDtypeStruct((sources, rows_local, width), jnp.bfloat16),
        ],
        compiler_params=pltpu.CompilerParams(vmem_limit_bytes=small_vmem),
    )(parts)


def terms_kernel(
    mixed_ref, residual_ref, gain_ref, gate_ref, up_ref, *rest, first, block, offset, sources
):
    if first:
        stream_ref, rest = rest[0], rest[1:]
    keep_ref, give_ref, normed = rest
    step = pl.program_id(0)
    upper = lax.rem(lax.axis_index("ctx"), 2) == 1
    rows_local = keep_ref.shape[1]

    def put(place, terms):
        for pair in range(sources // 2):
            begin = 2 * pair * rows_local
            low = terms[begin : begin + rows_local]
            high = terms[begin + rows_local : begin + 2 * rows_local]
            keep_ref[pair, :, place] = jnp.where(upper, high, low).astype(jnp.bfloat16)
            give_ref[pair, :, place] = jnp.where(upper, low, high).astype(jnp.bfloat16)

    @pl.when(step == 0)
    def start():
        combined = residual_ref[...].astype(jnp.float32) + mixed_ref[...]
        normed[...] = (combined * gain_ref[...]).astype(jnp.bfloat16)
        if first:
            stream_ref[...] = combined.astype(jnp.bfloat16)
            left = jnp.sum(combined * combined, axis=1, keepdims=True)
            spot = lax.broadcasted_iota(jnp.int32, (combined.shape[0], lane), 1)
            parts = jnp.zeros(spot.shape, jnp.float32)
            for piece in range(3):
                part = left.astype(jnp.bfloat16).astype(jnp.float32)
                parts = jnp.where(spot == piece, part, parts)
                left = left - part
            put(pl.ds(keep_ref.shape[2] - lane, lane), parts)

    begin = pl.multiple_of(step * 2 * block, lane)
    here = pl.ds(pl.multiple_of((step + offset) * block, lane), block)
    for place, weight_ref in ((begin, gate_ref), (begin + block, up_ref)):
        put(
            pl.ds(place, block),
            jnp.dot(normed[...], weight_ref[:, here], preferred_element_type=jnp.float32),
        )


def gate_and_up(mixed, residual, gain, w_gate, w_up, block, begin, end, sources):
    first = begin == 0
    rows, depth = residual.shape
    count = end - begin
    half = (sources // 2, rows // sources, 2 * block * count + (lane if first else 0))
    whole = lambda *shape: pl.BlockSpec(shape, lambda j: (0,) * len(shape))
    out_shape = [jax.ShapeDtypeStruct(half, jnp.bfloat16)] * 2
    out_specs = [whole(*half)] * 2
    if first:
        out_shape.insert(0, jax.ShapeDtypeStruct((rows, depth), jnp.bfloat16))
        out_specs.insert(0, whole(rows, depth))
    return pl.pallas_call(
        functools.partial(
            terms_kernel, first=first, block=block, offset=begin, sources=sources
        ),
        grid=(count,),
        in_specs=[
            whole(rows, depth),
            whole(rows, depth),
            whole(1, depth),
            pl.BlockSpec(memory_space=pltpu.VMEM),
            pl.BlockSpec(memory_space=pltpu.VMEM),
        ],
        out_specs=out_specs,
        out_shape=out_shape,
        scratch_shapes=[pltpu.VMEM((rows, depth), jnp.bfloat16)],
        compiler_params=pltpu.CompilerParams(
            dimension_semantics=("arbitrary",), vmem_limit_bytes=small_vmem
        ),
        cost_estimate=pl.CostEstimate(
            flops=4 * rows * depth * block * count,
            bytes_accessed=4 * depth * block * count,
            transcendentals=0,
        ),
    )(mixed, residual, gain[None], w_gate, w_up)


def hidden_kernel(terms_ref, copies_ref, *, block, counts, width):
    terms = [terms_ref[c].astype(jnp.float32) for c in range(terms_ref.shape[0])]
    terms = sum(terms)
    last = 2 * block * counts[0]
    square_total = terms[:, last : last + 1] + terms[:, last + 1 : last + 2]
    square_total = square_total + terms[:, last + 2 : last + 3]
    scale = lax.rsqrt(square_total / width + epsilon)
    place = 0
    begin = 0
    for index, count in enumerate(counts):
        for _ in range(count):
            gate = scale * terms[:, begin : begin + block]
            upward = scale * terms[:, begin + block : begin + 2 * block]
            hidden = (gate / (1.0 + jnp.exp(-gate)) * upward).astype(jnp.bfloat16)
            for c in range(copies_ref.shape[0]):
                copies_ref[c, :, place : place + block] = hidden
            place += block
            begin += 2 * block
        if index == 0:
            begin += lane


def hidden_copies(terms, block, counts, width, sources):
    shape = (sources, terms.shape[1], block * sum(counts))
    return pl.pallas_call(
        functools.partial(hidden_kernel, block=block, counts=counts, width=width),
        out_shape=jax.ShapeDtypeStruct(shape, jnp.bfloat16),
        compiler_params=pltpu.CompilerParams(vmem_limit_bytes=small_vmem),
    )(terms)


def give_half(total, keep_ref, give_ref, bit):
    upper = lax.rem(lax.div(lax.axis_index("head"), bit), 2) == 1
    half = keep_ref.shape[0]
    low, high = total[:half], total[half:]
    keep_ref[...] = jnp.where(upper, high, low)
    give_ref[...] = jnp.where(upper, low, high).astype(give_ref.dtype)


def halves(rows, columns, bit):
    sent = jnp.bfloat16 if bit > 1 else jnp.float32
    return [
        jax.ShapeDtypeStruct((rows // 2, columns), jnp.float32),
        jax.ShapeDtypeStruct((rows // 2, columns), sent),
    ]


def down_kernel(hidden_ref, weight_ref, keep_ref, give_ref, total_ref, *, bit):
    step = pl.program_id(0)

    @pl.when(step == 0)
    def start():
        total_ref[...] = jnp.zeros_like(total_ref)

    block = hidden_ref.shape[1]
    here = pl.ds(pl.multiple_of(step * block, lane), block)
    total_ref[...] += jnp.dot(
        hidden_ref[...], weight_ref[here], preferred_element_type=jnp.float32
    )

    @pl.when(step == pl.num_programs(0) - 1)
    def finish():
        give_half(total_ref[...], keep_ref, give_ref, bit)


def down(hidden, w_down, block, bit):
    rows, depth = hidden.shape
    columns = w_down.shape[1]
    out = halves(rows, columns, bit)
    return pl.pallas_call(
        functools.partial(down_kernel, bit=bit),
        grid=(depth // block,),
        in_specs=[
            pl.BlockSpec((rows, block), lambda j: (0, j)),
            pl.BlockSpec(memory_space=pltpu.VMEM),
        ],
        out_specs=[pl.BlockSpec(part.shape, lambda j: (0, 0)) for part in out],
        out_shape=out,
        scratch_shapes=[pltpu.VMEM((rows, columns), jnp.float32)],
        compiler_params=pltpu.CompilerParams(
            dimension_semantics=("arbitrary",), vmem_limit_bytes=small_vmem
        ),
        cost_estimate=pl.CostEstimate(
            flops=2 * rows * depth * columns, bytes_accessed=2 * depth * columns, transcendentals=0
        ),
    )(hidden, w_down)


def add_kernel(mine_ref, theirs_ref, keep_ref, give_ref, *, bit):
    give_half(mine_ref[...] + theirs_ref[...].astype(jnp.float32), keep_ref, give_ref, bit)


def add_and_split(mine, theirs, bit):
    return pl.pallas_call(
        functools.partial(add_kernel, bit=bit),
        out_shape=halves(*mine.shape, bit),
        compiler_params=pltpu.CompilerParams(vmem_limit_bytes=small_vmem),
    )(mine, theirs)


def spread(copies):
    gathered = lax.all_to_all(copies, "ctx", split_axis=0, concat_axis=0)
    return gathered.reshape((-1,) + copies.shape[2:])


def swap(block, axis, size, bit):
    return lax.ppermute(block, axis, [(i, i ^ bit) for i in range(size)])


def sum_over_head(block, size):
    bit = 1
    while bit < size:
        if bit > 1:
            block = block.astype(jnp.bfloat16)
        block = block.astype(jnp.float32) + swap(block, "head", size, bit).astype(jnp.float32)
        bit *= 2
    return block


def down_and_scatter(hidden, w_down, block, size):
    bit = size // 2
    keep, give = down(hidden, w_down, block, bit)
    while bit > 1:
        theirs = swap(give, "head", size, bit)
        bit //= 2
        keep, give = add_and_split(keep, theirs, bit)
    return keep + swap(give, "head", size, bit)


def local_step(sources, heads):
    def local(
        queries, keys, values, offsets, lengths, residual, wo, norm_gain, w_gate, w_up, w_down
    ):
        head_size = keys.shape[2]
        kv_local = keys.shape[1]
        rows_local = queries.shape[0]
        groups = queries.shape[1] // (kv_local * head_size)
        batch = lengths.shape[0]
        width = residual.shape[1] * sources
        everyone = spread(jnp.broadcast_to(queries[None], (sources,) + queries.shape))
        extra = -(-(batch + 1) // lane) * lane
        column = jnp.arange(extra, dtype=jnp.int32)
        limits = jnp.where(
            column < batch,
            jnp.pad(lengths, (0, extra - batch)) - offsets[0],
            jnp.where(column == batch, -1, jnp.iinfo(jnp.int32).max),
        )
        parts, w_gate, w_up, w_down = attention(
            everyone, limits[None], keys, values, sources, groups, (w_gate, w_up, w_down)
        )
        parts = lax.all_to_all(parts, "ctx", split_axis=0, concat_axis=0)
        attended, copies = merge(parts, kv_local, groups)
        projected = jnp.dot(spread(copies), wo, preferred_element_type=jnp.float32)
        mixed = sum_over_head(projected, heads)
        units = w_gate.shape[1]
        block = math.gcd(units, 640)
        blocks = units // block
        cuts = (0, (blocks + 1) // 2, blocks)
        counts = tuple(end - begin for begin, end in zip(cuts, cuts[1:]))
        terms = []
        for begin, end in zip(cuts, cuts[1:]):
            outs = gate_and_up(
                mixed, residual, norm_gain, w_gate, w_up, block, begin, end, sources
            )
            if begin == 0:
                stream = outs[0]
            keep, give = outs[-2:]
            theirs = swap(give, "ctx", sources, 1)
            terms.append(
                (keep.astype(jnp.float32) + theirs.astype(jnp.float32)).astype(jnp.bfloat16)
            )
        terms = lax.all_to_all(
            jnp.concatenate(terms, axis=2),
            "ctx",
            split_axis=0,
            concat_axis=0,
            axis_index_groups=[[c for c in range(sources) if c % 2 == s] for s in range(2)],
        )
        hidden = spread(hidden_copies(terms, block, counts, width, sources))
        ffn_out = down_and_scatter(hidden, w_down, block, heads)
        return (attended, stream, ffn_out.astype(jnp.bfloat16))

    return local


def solution(mesh):
    return jax.shard_map(
        local_step(mesh.shape["ctx"], mesh.shape["head"]),
        mesh=mesh,
        in_specs=(
            P("ctx", "head"),
            P("ctx", "head", None),
            P("ctx", "head", None),
            P("ctx"),
            P(),
            P(None, "ctx"),
            P("head", "ctx"),
            P("ctx"),
            P("ctx", "head"),
            P("ctx", "head"),
            P("head", "ctx"),
        ),
        out_specs=(P("ctx", "head"), P(None, "ctx"), P("head", "ctx")),
        check_vma=False,
    )
```

```python
import functools
import math

import jax
import jax.numpy as jnp
from jax import lax
from jax.experimental import pallas as pl
from jax.experimental.pallas import tpu as pltpu
from jax.sharding import PartitionSpec as P

hidden_score = -1e30
lowest_base = -65536.0
largest_sum = 2.0**115
epsilon = 1e-06
lane = 128
stat_rows = 16
attention_vmem = 32 * 2**20
most_vmem = 56 * 2**20
small_vmem = 8 * 2**20


def split_heads(block, kv_local, head_size):
    flat = block.reshape(block.shape[0], kv_local * head_size)
    return [flat[:, h * head_size : (h + 1) * head_size] for h in range(kv_local)]


def hidden_slots(first_slot, count, limits):
    slot = lax.broadcasted_iota(jnp.int32, (count, limits.shape[1]), 0) + first_slot
    return jnp.where(slot < limits, 0.0, 1.0).astype(jnp.bfloat16)


def scores_of(key_block, hidden, query_cols):
    return jnp.dot(
        jnp.concatenate([key_block, hidden], axis=1), query_cols, preferred_element_type=jnp.float32
    )


def weighted_values(value_block, weights):
    return lax.dot_general(
        value_block,
        weights.astype(jnp.bfloat16),
        (((0,), (0,)), ((), ())),
        preferred_element_type=jnp.float32,
    )


def sublane_sums(weights):
    return jnp.sum(weights.reshape(weights.shape[0] // 8, 8, weights.shape[1]), axis=0)


def query_kernel(*refs, kv_local, groups, pieces):
    piece_refs, (limit_ref, key_ref, cols_ref, base_ref, query_ref) = refs[:pieces], refs[pieces:]
    me = lax.axis_index("ctx")
    upper = lax.rem(me, 2) == 1
    pair_rows = piece_refs[0].shape[0]
    half = pair_rows // 2
    for distance, piece_ref in enumerate(piece_refs):
        piece = piece_ref[...].astype(jnp.float32)
        low = jnp.where(upper, piece[half:], piece[:half])
        high = jnp.where(upper, piece[:half], piece[half:])
        place = pl.multiple_of(lax.bitwise_xor(lax.div(me, 2), distance) * pair_rows, pair_rows)
        query_ref[pl.ds(place, pair_rows)] = jnp.concatenate([low, high], axis=0)
    batch = query_ref.shape[0]
    head_size = key_ref.shape[2]
    columns = batch * groups
    extra = limit_ref.shape[1]
    row = lax.broadcasted_iota(jnp.int32, (extra, columns), 0)
    column = lax.broadcasted_iota(jnp.int32, (extra, columns), 1)
    mask_rows = jnp.where(lax.rem(column, batch) == row, hidden_score, 0.0)
    hidden = hidden_slots(0, key_ref.shape[0], limit_ref[...])
    keys = split_heads(key_ref[...], kv_local, head_size)
    for h in range(kv_local):
        rows = [
            query_ref[:, (h * groups + g) * head_size : (h * groups + g + 1) * head_size]
            for g in range(groups)
        ]
        turned = jnp.concatenate(rows, axis=0).T
        cols_ref[h, :head_size] = turned.astype(jnp.bfloat16)
        cols_ref[h, head_size:] = mask_rows.astype(jnp.bfloat16)
        top = jnp.max(scores_of(keys[h], hidden, cols_ref[h]), axis=0, keepdims=True)
        base = jnp.maximum(top, lowest_base).astype(jnp.bfloat16).astype(jnp.float32)
        base_ref[h] = base
        cols_ref[h, head_size:] = jnp.where(row == batch, -base, mask_rows).astype(jnp.bfloat16)


def attention_kernel(
    query_cols,
    first_base,
    limit_ref,
    key_ref,
    value_ref,
    all_keys,
    all_values,
    *rest,
    kv_local,
    groups,
    sources,
    factor,
    carried,
):
    weights_in, rest = rest[:carried], rest[carried:]
    out_ref, weights_out, rest = rest[0], rest[1 : 1 + carried], rest[1 + carried :]
    (
    base_ref,
    acc_ref,
    total_ref,
    plain_cols,
    spare_keys,
    spare_values,
    copy_sems,
    weight_sems,
    ) = rest
    step = pl.program_id(0)
    head_size = key_ref.shape[2]
    block = key_ref.shape[0]
    columns = query_cols.shape[2]
    batch = columns // groups
    extra = limit_ref.shape[1]
    limits = limit_ref[...]
    steps = all_keys.shape[0] // block

    turns = [
        max(t for t in range(1, steps + 1) if weight.shape[0] % (16 * t) == 0)
        for weight in weights_in
    ]

    def weight_copies(index, turn):
        rows = weights_in[index].shape[0] // turns[index]
        here = pl.ds(pl.multiple_of(turn * rows, 16), rows)
        return pltpu.make_async_copy(
            weights_in[index].at[here], weights_out[index].at[here], weight_sems.at[index, turn]
        )

    for index in range(carried):
        pl.when(step < turns[index])(weight_copies(index, step).start)

    @pl.when(step == 0)
    def start():
        base_ref[...] = first_base[...]
        acc_ref[...] = jnp.zeros_like(acc_ref)
        total_ref[...] = jnp.zeros_like(total_ref)

    hidden = hidden_slots(step * block, block, limits)
    keys = split_heads(key_ref[...], kv_local, head_size)
    values = split_heads(value_ref[...], kv_local, head_size)
    for h in range(kv_local):
        weights = jnp.exp2(scores_of(keys[h], hidden, query_cols[h]) * factor)
        total_ref[h] += sublane_sums(weights)
        acc_ref[h] += weighted_values(values[h], weights)

    @pl.when(step == pl.num_programs(0) - 1)
    def finish():
        @pl.when(jnp.logical_not(jnp.max(total_ref[...]) <= largest_sum))
        def redo():
            piece = spare_keys.shape[0]
            row = lax.broadcasted_iota(jnp.int32, (head_size + extra, columns), 0)
            for h in range(kv_local):
                old = query_cols[h].astype(jnp.float32)
                plain_cols[h] = jnp.where(row == head_size + batch, 0.0, old).astype(jnp.bfloat16)
            base_ref[...] = jnp.full_like(base_ref, lowest_base)
            acc_ref[...] = jnp.zeros_like(acc_ref)
            total_ref[...] = jnp.zeros_like(total_ref)

            def visit(turn, carry):
                first = turn * piece
                here = pl.ds(first, piece)
                get_keys = pltpu.make_async_copy(all_keys.at[here], spare_keys, copy_sems.at[0])
                get_values = pltpu.make_async_copy(
                    all_values.at[here], spare_values, copy_sems.at[1]
                )
                get_keys.start()
                get_values.start()
                get_keys.wait()
                get_values.wait()
                hidden = hidden_slots(first, piece, limits)
                keys = split_heads(spare_keys[...], kv_local, head_size)
                values = split_heads(spare_values[...], kv_local, head_size)
                for h in range(kv_local):
                    scores = scores_of(keys[h], hidden, plain_cols[h])
                    old = base_ref[h]
                    new = jnp.maximum(old, jnp.max(scores, axis=0, keepdims=True))
                    rescale = jnp.exp2((old - new) * factor)
                    weights = jnp.exp2((scores - new) * factor)
                    base_ref[h] = new
                    total_ref[h] = total_ref[h] * rescale + sublane_sums(weights)
                    acc_ref[h] = acc_ref[h] * rescale + weighted_values(values[h], weights)
                return carry

            lax.fori_loop(0, all_keys.shape[0] // piece, visit, 0)

        for index in range(carried):
            for turn in range(turns[index]):
                weight_copies(index, turn).wait()
        rows_local = batch // sources
        rows = groups * rows_local
        stats = jnp.zeros((stat_rows, columns), jnp.float32)
        stat_row = lax.broadcasted_iota(jnp.int32, (stat_rows, columns), 0)
        for h in range(kv_local):
            total = jnp.sum(total_ref[h], axis=0, keepdims=True)
            seen = total > 0.0
            safe = jnp.where(seen, total, 1.0)
            height = jnp.where(seen, base_ref[h] * factor + jnp.log2(safe), hidden_score)
            for piece in range(3):
                part = height.astype(jnp.bfloat16).astype(jnp.float32)
                stats = jnp.where(stat_row == 3 * h + piece, part, stats)
                height = height - part
            mean = (acc_ref[h] * (1.0 / safe)).T.astype(jnp.bfloat16)
            for c in range(sources):
                for g in range(groups):
                    out_ref[c, h * rows + g * rows_local : h * rows + (g + 1) * rows_local] = mean[
                        g * batch + c * rows_local : g * batch + (c + 1) * rows_local
                    ]
        here = lax.broadcasted_iota(jnp.int32, (columns, columns), 0)
        there = lax.broadcasted_iota(jnp.int32, (columns, columns), 1)
        source, place = lax.div(there, rows), lax.rem(there, rows)
        origin = lax.div(place, rows_local) * batch + source * rows_local + lax.rem(place, rows_local)
        stats = jnp.dot(
            stats.astype(jnp.bfloat16),
            jnp.where(here == origin, 1.0, 0.0).astype(jnp.bfloat16),
            preferred_element_type=jnp.float32,
        )
        for c in range(sources):
            out_ref[c, kv_local * rows :, :rows] = stats[:, c * rows : (c + 1) * rows].astype(
                jnp.bfloat16
            )


def attention(pieces, limits, keys, values, sources, groups, weights=()):
    span, kv_local, head_size = keys.shape
    batch = len(pieces) * pieces[0].shape[0]
    columns = batch * groups
    block = math.gcd(4096, span)
    piece = math.gcd(1024, span)
    extra = limits.shape[1]
    whole = lambda *shape: pl.BlockSpec(shape, lambda j: (0,) * len(shape))
    part = pl.BlockSpec((block, kv_local, head_size), lambda j: (j, 0, 0))
    out = (sources, kv_local * columns // sources + stat_rows, head_size)
    depth = head_size + extra
    probe = math.gcd(512, span)
    query_cols, base = pl.pallas_call(
        functools.partial(
            query_kernel, kv_local=kv_local, groups=groups, pieces=len(pieces)
        ),
        grid=(1,),
        in_specs=[
            *[whole(*piece.shape) for piece in pieces],
            whole(1, extra),
            pl.BlockSpec((probe, kv_local, head_size), lambda j: (0, 0, 0)),
        ],
        out_specs=[whole(kv_local, depth, columns), whole(kv_local, 1, columns)],
        out_shape=[
            jax.ShapeDtypeStruct((kv_local, depth, columns), jnp.bfloat16),
            jax.ShapeDtypeStruct((kv_local, 1, columns), jnp.float32),
        ],
        scratch_shapes=[pltpu.VMEM((batch, pieces[0].shape[1]), jnp.float32)],
        compiler_params=pltpu.CompilerParams(vmem_limit_bytes=most_vmem),
    )(*pieces, limits, keys)
    return pl.pallas_call(
        functools.partial(
            attention_kernel,
            kv_local=kv_local,
            groups=groups,
            sources=sources,
            factor=math.log2(math.e) / math.sqrt(head_size),
            carried=len(weights),
        ),
        grid=(span // block,),
        in_specs=[
            whole(kv_local, depth, columns),
            whole(kv_local, 1, columns),
            whole(1, extra),
            part,
            part,
            pl.BlockSpec(memory_space=pl.ANY),
            pl.BlockSpec(memory_space=pl.ANY),
        ]
        + [pl.BlockSpec(memory_space=pl.ANY)] * len(weights),
        out_specs=[whole(*out)] + [pl.BlockSpec(memory_space=pltpu.VMEM)] * len(weights),
        out_shape=[jax.ShapeDtypeStruct(out, jnp.bfloat16)]
        + [pltpu.VMEM(weight.shape, weight.dtype) for weight in weights],
        scratch_shapes=[
            pltpu.VMEM((kv_local, 1, columns), jnp.float32),
            pltpu.VMEM((kv_local, head_size, columns), jnp.float32),
            pltpu.VMEM((kv_local, 8, columns), jnp.float32),
            pltpu.VMEM((kv_local, head_size + extra, columns), jnp.bfloat16),
            pltpu.VMEM((piece, kv_local, head_size), jnp.bfloat16),
            pltpu.VMEM((piece, kv_local, head_size), jnp.bfloat16),
            pltpu.SemaphoreType.DMA((2,)),
            pltpu.SemaphoreType.DMA((len(weights), span // block)),
        ],
        compiler_params=pltpu.CompilerParams(
            dimension_semantics=("arbitrary",), vmem_limit_bytes=attention_vmem
        ),
        cost_estimate=pl.CostEstimate(
            flops=4 * span * columns * kv_local * head_size,
            bytes_accessed=4 * span * kv_local * head_size,
            transcendentals=span * columns * kv_local,
        ),
    )(query_cols, base, limits, keys, values, keys, values, *weights)


def merge_kernel(part_ref, out_ref, copies_ref, *, kv_local, groups):
    sources, depth, head_size = part_ref.shape
    rows = (depth - stat_rows) // kv_local
    rows_local = rows // groups
    stats = part_ref[:, kv_local * rows :].astype(jnp.float32)
    stats = stats.reshape(sources * stat_rows, head_size).T
    for h in range(kv_local):
        heights = []
        for c in range(sources):
            first = c * stat_rows + 3 * h
            heights.append(
                stats[:rows, first : first + 1]
                + stats[:rows, first + 1 : first + 2]
                + stats[:rows, first + 2 : first + 3]
            )
        top = functools.reduce(jnp.maximum, heights)
        shares = [jnp.exp2(height - top) for height in heights]
        whole = sum(shares)
        mean = (
            sum(
                share * part_ref[c, h * rows : (h + 1) * rows].astype(jnp.float32)
                for c, share in enumerate(shares)
            )
            / whole
        )
        for g in range(groups):
            out_ref[:, (h * groups + g) * head_size : (h * groups + g + 1) * head_size] = mean[
                g * rows_local : (g + 1) * rows_local
            ].astype(jnp.bfloat16)
    copies_ref[...] = jnp.broadcast_to(out_ref[...][None], copies_ref.shape)


def merge(parts, kv_local, groups):
    sources, depth, head_size = parts.shape
    rows_local = (depth - stat_rows) // kv_local // groups
    width = kv_local * groups * head_size
    return pl.pallas_call(
        functools.partial(merge_kernel, kv_local=kv_local, groups=groups),
        out_shape=[
            jax.ShapeDtypeStruct((rows_local, width), jnp.bfloat16),
            jax.ShapeDtypeStruct((sources, rows_local, width), jnp.bfloat16),
        ],
        compiler_params=pltpu.CompilerParams(vmem_limit_bytes=small_vmem),
    )(parts)


def terms_kernel(
    mixed_ref, residual_ref, gain_ref, gate_ref, up_ref, *rest, first, block, offset, sources
):
    if first:
        stream_ref, rest = rest[0], rest[1:]
    keep_ref, give_ref, normed = rest
    step = pl.program_id(0)
    upper = lax.rem(lax.axis_index("ctx"), 2) == 1
    rows_local = keep_ref.shape[1]

    def put(place, terms):
        for pair in range(sources // 2):
            begin = 2 * pair * rows_local
            low = terms[begin : begin + rows_local]
            high = terms[begin + rows_local : begin + 2 * rows_local]
            keep_ref[pair, :, place] = jnp.where(upper, high, low).astype(jnp.bfloat16)
            give_ref[pair, :, place] = jnp.where(upper, low, high).astype(jnp.bfloat16)

    @pl.when(step == 0)
    def start():
        combined = residual_ref[...].astype(jnp.float32) + mixed_ref[...]
        normed[...] = (combined * gain_ref[...]).astype(jnp.bfloat16)
        if first:
            stream_ref[...] = combined.astype(jnp.bfloat16)
        left = jnp.sum(combined * combined, axis=1, keepdims=True)
        spot = lax.broadcasted_iota(jnp.int32, (combined.shape[0], lane), 1)
        parts = jnp.zeros(spot.shape, jnp.float32)
        for piece in range(3):
            part = left.astype(jnp.bfloat16).astype(jnp.float32)
            parts = jnp.where(spot == piece, part, parts)
            left = left - part
        put(pl.ds(keep_ref.shape[2] - lane, lane), parts)

    begin = pl.multiple_of(step * 2 * block, lane)
    here = pl.ds(pl.multiple_of((step + offset) * block, lane), block)
    for place, weight_ref in ((begin, gate_ref), (begin + block, up_ref)):
        put(
            pl.ds(place, block),
            jnp.dot(normed[...], weight_ref[:, here], preferred_element_type=jnp.float32),
        )


def gate_and_up(mixed, residual, gain, w_gate, w_up, block, begin, end, sources):
    first = begin == 0
    rows, depth = residual.shape
    count = end - begin
    half = (sources // 2, rows // sources, 2 * block * count + lane)
    whole = lambda *shape: pl.BlockSpec(shape, lambda j: (0,) * len(shape))
    out_shape = [jax.ShapeDtypeStruct(half, jnp.bfloat16)] * 2
    out_specs = [whole(*half)] * 2
    if first:
        out_shape.insert(0, jax.ShapeDtypeStruct((rows, depth), jnp.bfloat16))
        out_specs.insert(0, whole(rows, depth))
    return pl.pallas_call(
        functools.partial(
            terms_kernel, first=first, block=block, offset=begin, sources=sources
        ),
        grid=(count,),
        in_specs=[
            whole(rows, depth),
            whole(rows, depth),
            whole(1, depth),
            pl.BlockSpec(memory_space=pltpu.VMEM),
            pl.BlockSpec(memory_space=pltpu.VMEM),
        ],
        out_specs=out_specs,
        out_shape=out_shape,
        scratch_shapes=[pltpu.VMEM((rows, depth), jnp.bfloat16)],
        compiler_params=pltpu.CompilerParams(
            dimension_semantics=("arbitrary",), vmem_limit_bytes=small_vmem
        ),
        cost_estimate=pl.CostEstimate(
            flops=4 * rows * depth * block * count,
            bytes_accessed=4 * depth * block * count,
            transcendentals=0,
        ),
    )(mixed, residual, gain[None], w_gate, w_up)


def pair_kernel(keep_ref, theirs_ref, *out_refs):
    mine = lax.div(lax.axis_index("ctx"), 2)
    for distance, out_ref in enumerate(out_refs):
        pair = lax.bitwise_xor(mine, distance)
        total = keep_ref[pair].astype(jnp.float32) + theirs_ref[pair].astype(jnp.float32)
        out_ref[...] = total.astype(jnp.bfloat16)


def pair_sums(keep, theirs):
    return pl.pallas_call(
        pair_kernel,
        out_shape=[jax.ShapeDtypeStruct(keep.shape[1:], jnp.bfloat16)] * keep.shape[0],
        compiler_params=pltpu.CompilerParams(vmem_limit_bytes=small_vmem),
    )(keep, theirs)


def hidden_kernel(*refs, block, width):
    out_ref = refs[-1]
    terms = sum(part[...].astype(jnp.float32) for part in refs[:-1])
    last = terms.shape[1] - lane
    square_total = terms[:, last : last + 1] + terms[:, last + 1 : last + 2]
    square_total = square_total + terms[:, last + 2 : last + 3]
    scale = lax.rsqrt(square_total / width + epsilon)
    for begin in range(0, last, 2 * block):
        gate = scale * terms[:, begin : begin + block]
        upward = scale * terms[:, begin + block : begin + 2 * block]
        hidden = gate / (1.0 + jnp.exp(-gate)) * upward
        out_ref[:, begin // 2 : begin // 2 + block] = hidden.astype(jnp.bfloat16)


def hidden_units(parts, block, width):
    shape = (parts[0].shape[0], (parts[0].shape[1] - lane) // 2)
    return pl.pallas_call(
        functools.partial(hidden_kernel, block=block, width=width),
        out_shape=jax.ShapeDtypeStruct(shape, jnp.bfloat16),
        compiler_params=pltpu.CompilerParams(vmem_limit_bytes=small_vmem),
    )(*parts)


def give_half(total, keep_ref, give_ref, bit):
    upper = lax.rem(lax.div(lax.axis_index("head"), bit), 2) == 1
    half = keep_ref.shape[0]
    low, high = total[:half], total[half:]
    keep_ref[...] = jnp.where(upper, high, low)
    give_ref[...] = jnp.where(upper, low, high).astype(give_ref.dtype)


def halves(rows, columns, bit):
    sent = jnp.bfloat16 if bit > 1 else jnp.float32
    return [
        jax.ShapeDtypeStruct((rows // 2, columns), jnp.float32),
        jax.ShapeDtypeStruct((rows // 2, columns), sent),
    ]


def down_kernel(mine_ref, theirs_ref, weight_ref, *refs, offset, started, finished, rows_local, bit):
    if started:
        before_ref, refs = refs[0], refs[1:]
    if finished:
        keep_ref, give_ref, total_ref, ordered_ref = refs
    else:
        (total_ref,) = refs
    step = pl.program_id(0)

    @pl.when(step == 0)
    def start():
        total_ref[...] = before_ref[...] if started else jnp.zeros_like(total_ref)

    block = mine_ref.shape[1]
    here = pl.ds(pl.multiple_of((step + offset) * block, lane), block)
    total_ref[...] += jnp.dot(
        jnp.concatenate([mine_ref[...], theirs_ref[...]], axis=0),
        weight_ref[here],
        preferred_element_type=jnp.float32,
    )

    if finished:

        @pl.when(step == pl.num_programs(0) - 1)
        def finish():
            me = lax.axis_index("ctx")
            pairs = ordered_ref.shape[0] // 2
            for other in range(2):
                side = lax.bitwise_xor(lax.rem(me, 2), other)
                for distance in range(pairs):
                    pair = lax.bitwise_xor(lax.div(me, 2), distance)
                    begin = (other * pairs + distance) * rows_local
                    ordered_ref[2 * pair + side] = total_ref[begin : begin + rows_local]
            give_half(ordered_ref[...].reshape(total_ref.shape), keep_ref, give_ref, bit)


def down(mine, theirs, w_down, before, block, begin, finished, rows_local, bit):
    half, depth = mine.shape
    rows, columns = 2 * half, w_down.shape[1]
    operands = [mine, theirs, w_down]
    in_specs = [pl.BlockSpec((half, block), lambda j: (0, j))] * 2
    in_specs.append(pl.BlockSpec(memory_space=pltpu.VMEM))
    if before is not None:
        operands.append(before)
        in_specs.append(pl.BlockSpec((rows, columns), lambda j: (0, 0)))
    if finished:
        out = halves(rows, columns, bit)
        scratch = [
            pltpu.VMEM((rows, columns), jnp.float32),
            pltpu.VMEM((rows // rows_local, rows_local, columns), jnp.float32),
        ]
    else:
        out = [jax.ShapeDtypeStruct((rows, columns), jnp.float32)]
        scratch = []
    return pl.pallas_call(
        functools.partial(
            down_kernel,
            offset=begin,
            started=before is not None,
            finished=finished,
            rows_local=rows_local,
            bit=bit,
        ),
        grid=(depth // block,),
        in_specs=in_specs,
        out_specs=[pl.BlockSpec(part.shape, lambda j: (0, 0)) for part in out],
        out_shape=out,
        scratch_shapes=scratch,
        compiler_params=pltpu.CompilerParams(
            dimension_semantics=("arbitrary",), vmem_limit_bytes=small_vmem
        ),
        cost_estimate=pl.CostEstimate(
            flops=2 * rows * depth * columns, bytes_accessed=2 * depth * columns, transcendentals=0
        ),
    )(*operands)


def add_kernel(mine_ref, theirs_ref, keep_ref, give_ref, *, bit):
    give_half(mine_ref[...] + theirs_ref[...].astype(jnp.float32), keep_ref, give_ref, bit)


def add_and_split(mine, theirs, bit):
    return pl.pallas_call(
        functools.partial(add_kernel, bit=bit),
        out_shape=halves(*mine.shape, bit),
        compiler_params=pltpu.CompilerParams(vmem_limit_bytes=small_vmem),
    )(mine, theirs)


def spread(copies):
    gathered = lax.all_to_all(copies, "ctx", split_axis=0, concat_axis=0)
    return gathered.reshape((-1,) + copies.shape[2:])


def swap(block, axis, size, bit):
    return lax.ppermute(block, axis, [(i, i ^ bit) for i in range(size)])


def sum_over_head(block, size):
    bit = 1
    while bit < size:
        if bit > 1:
            block = block.astype(jnp.bfloat16)
        block = block.astype(jnp.float32) + swap(block, "head", size, bit).astype(jnp.float32)
        bit *= 2
    return block


def scatter_over_head(keep, give, size):
    bit = size // 2
    while bit > 1:
        theirs = swap(give, "head", size, bit)
        bit //= 2
        keep, give = add_and_split(keep, theirs, bit)
    return keep + swap(give, "head", size, bit)


def local_step(sources, heads):
    def local(
        queries, keys, values, offsets, lengths, residual, wo, norm_gain, w_gate, w_up, w_down
    ):
        head_size = keys.shape[2]
        kv_local = keys.shape[1]
        rows_local = queries.shape[0]
        groups = queries.shape[1] // (kv_local * head_size)
        batch = lengths.shape[0]
        width = residual.shape[1] * sources
        pair = jnp.concatenate([queries, swap(queries, "ctx", sources, 1)], axis=0)
        pieces = [pair] + [swap(pair, "ctx", sources, 2 * d) for d in range(1, sources // 2)]
        extra = -(-(batch + 1) // lane) * lane
        column = jnp.arange(extra, dtype=jnp.int32)
        limits = jnp.where(
            column < batch,
            jnp.pad(lengths, (0, extra - batch)) - offsets[0],
            jnp.where(column == batch, -1, jnp.iinfo(jnp.int32).max),
        )
        parts, w_gate, w_up, w_down = attention(
            pieces, limits[None], keys, values, sources, groups, (w_gate, w_up, w_down)
        )
        parts = lax.all_to_all(parts, "ctx", split_axis=0, concat_axis=0)
        attended, copies = merge(parts, kv_local, groups)
        projected = jnp.dot(spread(copies), wo, preferred_element_type=jnp.float32)
        mixed = sum_over_head(projected, heads)
        units = w_gate.shape[1]
        block = math.gcd(units, 640)
        blocks = units // block
        cuts = sorted({0, blocks} | {blocks * part // 100 for part in (50,)})
        counts = tuple(end - begin for begin, end in zip(cuts, cuts[1:]))
        chunks = []
        for begin, end in zip(cuts, cuts[1:]):
            outs = gate_and_up(
                mixed, residual, norm_gain, w_gate, w_up, block, begin, end, sources
            )
            if begin == 0:
                stream = outs[0]
            chunks.append(outs[-2:])
        terms = []
        for keep, give in chunks:
            sums = pair_sums(keep, swap(give, "ctx", sources, 1))
            terms.append(
                [sums[0]] + [swap(sums[d], "ctx", sources, 2 * d) for d in range(1, len(sums))]
            )
        total = None
        for parts, begin, end in zip(terms, cuts, cuts[1:]):
            own = hidden_units(parts, block, width)
            mine = jnp.concatenate(
                [own] + [swap(own, "ctx", sources, 2 * d) for d in range(1, sources // 2)], axis=0
            )
            theirs = swap(mine, "ctx", sources, 1)
            total = down(
                mine, theirs, w_down, total, block, begin, end == blocks, rows_local, heads // 2
            )
            if end < blocks:
                (total,) = total
        ffn_out = scatter_over_head(*total, heads)
        return (attended, stream, ffn_out.astype(jnp.bfloat16))

    return local


def solution(mesh):
    return jax.shard_map(
        local_step(mesh.shape["ctx"], mesh.shape["head"]),
        mesh=mesh,
        in_specs=(
            P("ctx", "head"),
            P("ctx", "head", None),
            P("ctx", "head", None),
            P("ctx"),
            P(),
            P(None, "ctx"),
            P("head", "ctx"),
            P("ctx"),
            P("ctx", "head"),
            P("ctx", "head"),
            P("head", "ctx"),
        ),
        out_specs=(P("ctx", "head"), P(None, "ctx"), P("head", "ctx")),
        check_vma=False,
    )
```

```python
import functools
import math

import jax
import jax.numpy as jnp
from jax import lax
from jax.experimental import pallas as pl
from jax.experimental.pallas import tpu as pltpu
from jax.sharding import PartitionSpec as P

hidden_score = -1e30
lowest_base = -65536.0
largest_sum = 2.0**115
epsilon = 1e-06
lane = 128
stat_rows = 16
attention_vmem = 32 * 2**20
most_vmem = 56 * 2**20
small_vmem = 8 * 2**20


def split_heads(block, kv_local, head_size):
    flat = block.reshape(block.shape[0], kv_local * head_size)
    return [flat[:, h * head_size : (h + 1) * head_size] for h in range(kv_local)]


def hidden_slots(first_slot, count, limits):
    slot = lax.broadcasted_iota(jnp.int32, (count, limits.shape[1]), 0) + first_slot
    return jnp.where(slot < limits, 0.0, 1.0).astype(jnp.bfloat16)


def scores_of(key_block, hidden, query_cols):
    return jnp.dot(
        jnp.concatenate([key_block, hidden], axis=1), query_cols, preferred_element_type=jnp.float32
    )


def weighted_values(value_block, weights):
    return lax.dot_general(
        value_block,
        weights.astype(jnp.bfloat16),
        (((0,), (0,)), ((), ())),
        preferred_element_type=jnp.float32,
    )


def sublane_sums(weights):
    return jnp.sum(weights.reshape(weights.shape[0] // 8, 8, weights.shape[1]), axis=0)


def attention_kernel(
    *refs,
    pieces,
    kv_local,
    groups,
    sources,
    factor,
    carried,
):
    piece_refs, rest = refs[:pieces], refs[pieces:]
    probe_ref, length_ref, offset_ref, key_ref, value_ref, all_keys, all_values, *rest = rest
    weights_in, rest = rest[:carried], rest[carried:]
    out_ref, weights_out, rest = rest[0], rest[1 : 1 + carried], rest[1 + carried :]
    (
    query_ref,
    query_cols,
    base_ref,
    acc_ref,
    total_ref,
    plain_cols,
    spare_keys,
    spare_values,
    copy_sems,
    weight_sems,
    ) = rest
    step = pl.program_id(0)
    head_size = key_ref.shape[2]
    block = key_ref.shape[0]
    columns = query_cols.shape[2]
    batch = columns // groups
    extra = query_cols.shape[1] - head_size
    spot = lax.broadcasted_iota(jnp.int32, (1, extra), 1)
    ends = jnp.concatenate(
        [length_ref[...] - offset_ref[0], jnp.zeros((1, extra - batch), jnp.int32)], axis=1
    )
    limits = jnp.where(spot < batch, ends, jnp.where(spot == batch, -1, jnp.iinfo(jnp.int32).max))
    steps = all_keys.shape[0] // block

    turns = [
        max(t for t in range(1, steps + 1) if weight.shape[0] % (16 * t) == 0)
        for weight in weights_in
    ]

    def weight_copies(index, turn):
        rows = weights_in[index].shape[0] // turns[index]
        here = pl.ds(pl.multiple_of(turn * rows, 16), rows)
        return pltpu.make_async_copy(
            weights_in[index].at[here], weights_out[index].at[here], weight_sems.at[index, turn]
        )

    for index in range(carried):
        pl.when(step < turns[index])(weight_copies(index, step).start)

    @pl.when(step == 0)
    def start():
        me = lax.axis_index("ctx")
        upper = lax.rem(me, 2) == 1
        pair_rows = piece_refs[0].shape[0]
        half = pair_rows // 2
        for distance, piece_ref in enumerate(piece_refs):
            piece = piece_ref[...].astype(jnp.float32)
            low = jnp.where(upper, piece[half:], piece[:half])
            high = jnp.where(upper, piece[:half], piece[half:])
            place = pl.multiple_of(lax.bitwise_xor(lax.div(me, 2), distance) * pair_rows, pair_rows)
            query_ref[pl.ds(place, pair_rows)] = jnp.concatenate([low, high], axis=0)
        row = lax.broadcasted_iota(jnp.int32, (extra, columns), 0)
        column = lax.broadcasted_iota(jnp.int32, (extra, columns), 1)
        mask_rows = jnp.where(lax.rem(column, batch) == row, hidden_score, 0.0)
        hidden = hidden_slots(0, probe_ref.shape[0], limits)
        keys = split_heads(probe_ref[...], kv_local, head_size)
        for h in range(kv_local):
            rows = [
                query_ref[:, (h * groups + g) * head_size : (h * groups + g + 1) * head_size]
                for g in range(groups)
            ]
            turned = jnp.concatenate(rows, axis=0).T
            query_cols[h, :head_size] = turned.astype(jnp.bfloat16)
            query_cols[h, head_size:] = mask_rows.astype(jnp.bfloat16)
            top = jnp.max(scores_of(keys[h], hidden, query_cols[h]), axis=0, keepdims=True)
            base = jnp.maximum(top, lowest_base).astype(jnp.bfloat16).astype(jnp.float32)
            base_ref[h] = base
            query_cols[h, head_size:] = jnp.where(row == batch, -base, mask_rows).astype(jnp.bfloat16)
        acc_ref[...] = jnp.zeros_like(acc_ref)
        total_ref[...] = jnp.zeros_like(total_ref)

    hidden = hidden_slots(step * block, block, limits)
    keys = split_heads(key_ref[...], kv_local, head_size)
    values = split_heads(value_ref[...], kv_local, head_size)
    for h in range(kv_local):
        weights = jnp.exp2(scores_of(keys[h], hidden, query_cols[h]) * factor)
        total_ref[h] += sublane_sums(weights)
        acc_ref[h] += weighted_values(values[h], weights)

    @pl.when(step == pl.num_programs(0) - 1)
    def finish():
        @pl.when(jnp.logical_not(jnp.max(total_ref[...]) <= largest_sum))
        def redo():
            piece = spare_keys.shape[0]
            row = lax.broadcasted_iota(jnp.int32, (head_size + extra, columns), 0)
            for h in range(kv_local):
                old = query_cols[h].astype(jnp.float32)
                plain_cols[h] = jnp.where(row == head_size + batch, 0.0, old).astype(jnp.bfloat16)
            base_ref[...] = jnp.full_like(base_ref, lowest_base)
            acc_ref[...] = jnp.zeros_like(acc_ref)
            total_ref[...] = jnp.zeros_like(total_ref)

            def visit(turn, carry):
                first = turn * piece
                here = pl.ds(first, piece)
                get_keys = pltpu.make_async_copy(all_keys.at[here], spare_keys, copy_sems.at[0])
                get_values = pltpu.make_async_copy(
                    all_values.at[here], spare_values, copy_sems.at[1]
                )
                get_keys.start()
                get_values.start()
                get_keys.wait()
                get_values.wait()
                hidden = hidden_slots(first, piece, limits)
                keys = split_heads(spare_keys[...], kv_local, head_size)
                values = split_heads(spare_values[...], kv_local, head_size)
                for h in range(kv_local):
                    scores = scores_of(keys[h], hidden, plain_cols[h])
                    old = base_ref[h]
                    new = jnp.maximum(old, jnp.max(scores, axis=0, keepdims=True))
                    rescale = jnp.exp2((old - new) * factor)
                    weights = jnp.exp2((scores - new) * factor)
                    base_ref[h] = new
                    total_ref[h] = total_ref[h] * rescale + sublane_sums(weights)
                    acc_ref[h] = acc_ref[h] * rescale + weighted_values(values[h], weights)
                return carry

            lax.fori_loop(0, all_keys.shape[0] // piece, visit, 0)

        for index in range(carried):
            for turn in range(turns[index]):
                weight_copies(index, turn).wait()
        rows_local = batch // sources
        rows = groups * rows_local
        stats = jnp.zeros((stat_rows, columns), jnp.float32)
        stat_row = lax.broadcasted_iota(jnp.int32, (stat_rows, columns), 0)
        for h in range(kv_local):
            total = jnp.sum(total_ref[h], axis=0, keepdims=True)
            seen = total > 0.0
            safe = jnp.where(seen, total, 1.0)
            height = jnp.where(seen, base_ref[h] * factor + jnp.log2(safe), hidden_score)
            for piece in range(3):
                part = height.astype(jnp.bfloat16).astype(jnp.float32)
                stats = jnp.where(stat_row == 3 * h + piece, part, stats)
                height = height - part
            mean = (acc_ref[h] * (1.0 / safe)).T.astype(jnp.bfloat16)
            for c in range(sources):
                for g in range(groups):
                    out_ref[c, h * rows + g * rows_local : h * rows + (g + 1) * rows_local] = mean[
                        g * batch + c * rows_local : g * batch + (c + 1) * rows_local
                    ]
        here = lax.broadcasted_iota(jnp.int32, (columns, columns), 0)
        there = lax.broadcasted_iota(jnp.int32, (columns, columns), 1)
        source, place = lax.div(there, rows), lax.rem(there, rows)
        origin = lax.div(place, rows_local) * batch + source * rows_local + lax.rem(place, rows_local)
        stats = jnp.dot(
            stats.astype(jnp.bfloat16),
            jnp.where(here == origin, 1.0, 0.0).astype(jnp.bfloat16),
            preferred_element_type=jnp.float32,
        )
        for c in range(sources):
            out_ref[c, kv_local * rows :, :rows] = stats[:, c * rows : (c + 1) * rows].astype(
                jnp.bfloat16
            )


def attention(pieces, lengths, offsets, keys, values, sources, groups, weights=()):
    span, kv_local, head_size = keys.shape
    batch = len(pieces) * pieces[0].shape[0]
    columns = batch * groups
    block = math.gcd(4096, span)
    piece = math.gcd(1024, span)
    extra = -(-(batch + 1) // lane) * lane
    whole = lambda *shape: pl.BlockSpec(shape, lambda j: (0,) * len(shape))
    part = pl.BlockSpec((block, kv_local, head_size), lambda j: (j, 0, 0))
    out = (sources, kv_local * columns // sources + stat_rows, head_size)
    depth = head_size + extra
    probe = math.gcd(512, span)
    return pl.pallas_call(
        functools.partial(
            attention_kernel,
            pieces=len(pieces),
            kv_local=kv_local,
            groups=groups,
            sources=sources,
            factor=math.log2(math.e) / math.sqrt(head_size),
            carried=len(weights),
        ),
        grid=(span // block,),
        in_specs=[
            *[whole(*piece.shape) for piece in pieces],
            whole(probe, kv_local, head_size),
            whole(1, batch),
            pl.BlockSpec(memory_space=pltpu.SMEM),
            part,
            part,
            pl.BlockSpec(memory_space=pl.ANY),
            pl.BlockSpec(memory_space=pl.ANY),
        ]
        + [pl.BlockSpec(memory_space=pl.ANY)] * len(weights),
        out_specs=[whole(*out)] + [pl.BlockSpec(memory_space=pltpu.VMEM)] * len(weights),
        out_shape=[jax.ShapeDtypeStruct(out, jnp.bfloat16)]
        + [pltpu.VMEM(weight.shape, weight.dtype) for weight in weights],
        scratch_shapes=[
            pltpu.VMEM((batch, pieces[0].shape[1]), jnp.float32),
            pltpu.VMEM((kv_local, depth, columns), jnp.bfloat16),
            pltpu.VMEM((kv_local, 1, columns), jnp.float32),
            pltpu.VMEM((kv_local, head_size, columns), jnp.float32),
            pltpu.VMEM((kv_local, 8, columns), jnp.float32),
            pltpu.VMEM((kv_local, head_size + extra, columns), jnp.bfloat16),
            pltpu.VMEM((piece, kv_local, head_size), jnp.bfloat16),
            pltpu.VMEM((piece, kv_local, head_size), jnp.bfloat16),
            pltpu.SemaphoreType.DMA((2,)),
            pltpu.SemaphoreType.DMA((len(weights), span // block)),
        ],
        compiler_params=pltpu.CompilerParams(
            dimension_semantics=("arbitrary",), vmem_limit_bytes=attention_vmem
        ),
        cost_estimate=pl.CostEstimate(
            flops=4 * span * columns * kv_local * head_size,
            bytes_accessed=4 * span * kv_local * head_size,
            transcendentals=span * columns * kv_local,
        ),
    )(*pieces, keys, lengths[None], offsets, keys, values, keys, values, *weights)


def merge_kernel(part_ref, out_ref, copies_ref, *, kv_local, groups):
    sources, depth, head_size = part_ref.shape
    rows = (depth - stat_rows) // kv_local
    rows_local = rows // groups
    stats = part_ref[:, kv_local * rows :].astype(jnp.float32)
    stats = stats.reshape(sources * stat_rows, head_size).T
    for h in range(kv_local):
        heights = []
        for c in range(sources):
            first = c * stat_rows + 3 * h
            heights.append(
                stats[:rows, first : first + 1]
                + stats[:rows, first + 1 : first + 2]
                + stats[:rows, first + 2 : first + 3]
            )
        top = functools.reduce(jnp.maximum, heights)
        shares = [jnp.exp2(height - top) for height in heights]
        whole = sum(shares)
        mean = (
            sum(
                share * part_ref[c, h * rows : (h + 1) * rows].astype(jnp.float32)
                for c, share in enumerate(shares)
            )
            / whole
        )
        for g in range(groups):
            out_ref[:, (h * groups + g) * head_size : (h * groups + g + 1) * head_size] = mean[
                g * rows_local : (g + 1) * rows_local
            ].astype(jnp.bfloat16)
    copies_ref[...] = jnp.broadcast_to(out_ref[...][None], copies_ref.shape)


def merge(parts, kv_local, groups):
    sources, depth, head_size = parts.shape
    rows_local = (depth - stat_rows) // kv_local // groups
    width = kv_local * groups * head_size
    return pl.pallas_call(
        functools.partial(merge_kernel, kv_local=kv_local, groups=groups),
        out_specs=[pl.BlockSpec(memory_space=pltpu.VMEM)] * 2,
        out_shape=[
            pltpu.VMEM((rows_local, width), jnp.bfloat16),
            jax.ShapeDtypeStruct((sources, rows_local, width), jnp.bfloat16),
        ],
        compiler_params=pltpu.CompilerParams(vmem_limit_bytes=small_vmem),
    )(parts)


def terms_kernel(
    mixed_ref, residual_ref, gain_ref, gate_ref, up_ref, *rest, first, block, offset, sources
):
    if first:
        stream_ref, rest = rest[0], rest[1:]
    keep_ref, give_ref, normed = rest
    step = pl.program_id(0)
    upper = lax.rem(lax.axis_index("ctx"), 2) == 1
    rows_local = keep_ref.shape[1]

    def put(place, terms):
        for pair in range(sources // 2):
            begin = 2 * pair * rows_local
            low = terms[begin : begin + rows_local]
            high = terms[begin + rows_local : begin + 2 * rows_local]
            keep_ref[pair, :, place] = jnp.where(upper, high, low).astype(jnp.bfloat16)
            give_ref[pair, :, place] = jnp.where(upper, low, high).astype(jnp.bfloat16)

    @pl.when(step == 0)
    def start():
        combined = residual_ref[...].astype(jnp.float32) + mixed_ref[...]
        normed[...] = (combined * gain_ref[...]).astype(jnp.bfloat16)
        if first:
            stream_ref[...] = combined.astype(jnp.bfloat16)
        left = jnp.sum(combined * combined, axis=1, keepdims=True)
        spot = lax.broadcasted_iota(jnp.int32, (combined.shape[0], lane), 1)
        parts = jnp.zeros(spot.shape, jnp.float32)
        for piece in range(3):
            part = left.astype(jnp.bfloat16).astype(jnp.float32)
            parts = jnp.where(spot == piece, part, parts)
            left = left - part
        put(pl.ds(keep_ref.shape[2] - lane, lane), parts)

    begin = pl.multiple_of(step * 2 * block, lane)
    here = pl.ds(pl.multiple_of((step + offset) * block, lane), block)
    for place, weight_ref in ((begin, gate_ref), (begin + block, up_ref)):
        put(
            pl.ds(place, block),
            jnp.dot(normed[...], weight_ref[:, here], preferred_element_type=jnp.float32),
        )


def gate_and_up(mixed, residual, gain, w_gate, w_up, block, begin, end, sources):
    first = begin == 0
    rows, depth = residual.shape
    count = end - begin
    half = (sources // 2, rows // sources, 2 * block * count + lane)
    whole = lambda *shape: pl.BlockSpec(shape, lambda j: (0,) * len(shape))
    out_shape = [jax.ShapeDtypeStruct(half, jnp.bfloat16)] * 2
    out_specs = [whole(*half)] * 2
    if first:
        out_shape.insert(0, pltpu.VMEM((rows, depth), jnp.bfloat16))
        out_specs.insert(0, pl.BlockSpec(memory_space=pltpu.VMEM))
    return pl.pallas_call(
        functools.partial(
            terms_kernel, first=first, block=block, offset=begin, sources=sources
        ),
        grid=(count,),
        in_specs=[
            whole(rows, depth),
            whole(rows, depth),
            whole(1, depth),
            pl.BlockSpec(memory_space=pltpu.VMEM),
            pl.BlockSpec(memory_space=pltpu.VMEM),
        ],
        out_specs=out_specs,
        out_shape=out_shape,
        scratch_shapes=[pltpu.VMEM((rows, depth), jnp.bfloat16)],
        compiler_params=pltpu.CompilerParams(
            dimension_semantics=("arbitrary",), vmem_limit_bytes=small_vmem
        ),
        cost_estimate=pl.CostEstimate(
            flops=4 * rows * depth * block * count,
            bytes_accessed=4 * depth * block * count,
            transcendentals=0,
        ),
    )(mixed, residual, gain[None], w_gate, w_up)


def pair_kernel(keep_ref, theirs_ref, *out_refs):
    mine = lax.div(lax.axis_index("ctx"), 2)
    for distance, out_ref in enumerate(out_refs):
        pair = lax.bitwise_xor(mine, distance)
        total = keep_ref[pair].astype(jnp.float32) + theirs_ref[pair].astype(jnp.float32)
        out_ref[...] = total.astype(jnp.bfloat16)


def pair_sums(keep, theirs):
    return pl.pallas_call(
        pair_kernel,
        out_shape=[jax.ShapeDtypeStruct(keep.shape[1:], jnp.bfloat16)] * keep.shape[0],
        compiler_params=pltpu.CompilerParams(vmem_limit_bytes=small_vmem),
    )(keep, theirs)


def hidden_kernel(*refs, block, width):
    out_ref = refs[-1]
    terms = sum(part[...].astype(jnp.float32) for part in refs[:-1])
    last = terms.shape[1] - lane
    square_total = terms[:, last : last + 1] + terms[:, last + 1 : last + 2]
    square_total = square_total + terms[:, last + 2 : last + 3]
    scale = lax.rsqrt(square_total / width + epsilon)
    for begin in range(0, last, 2 * block):
        gate = scale * terms[:, begin : begin + block]
        upward = scale * terms[:, begin + block : begin + 2 * block]
        hidden = gate / (1.0 + jnp.exp(-gate)) * upward
        out_ref[:, begin // 2 : begin // 2 + block] = hidden.astype(jnp.bfloat16)


def hidden_units(parts, block, width):
    shape = (parts[0].shape[0], (parts[0].shape[1] - lane) // 2)
    return pl.pallas_call(
        functools.partial(hidden_kernel, block=block, width=width),
        out_shape=jax.ShapeDtypeStruct(shape, jnp.bfloat16),
        compiler_params=pltpu.CompilerParams(vmem_limit_bytes=small_vmem),
    )(*parts)


def give_half(total, keep_ref, give_ref, bit):
    upper = lax.rem(lax.div(lax.axis_index("head"), bit), 2) == 1
    half = keep_ref.shape[0]
    low, high = total[:half], total[half:]
    keep_ref[...] = jnp.where(upper, high, low)
    give_ref[...] = jnp.where(upper, low, high).astype(give_ref.dtype)


def halves(rows, columns, bit):
    sent = jnp.bfloat16 if bit > 1 else jnp.float32
    return [
        jax.ShapeDtypeStruct((rows // 2, columns), jnp.float32),
        jax.ShapeDtypeStruct((rows // 2, columns), sent),
    ]


def down_kernel(mine_ref, theirs_ref, weight_ref, *refs, offset, started, finished, rows_local, bit):
    if started:
        before_ref, refs = refs[0], refs[1:]
    if finished:
        keep_ref, give_ref, total_ref, ordered_ref = refs
    else:
        (total_ref,) = refs
    step = pl.program_id(0)

    @pl.when(step == 0)
    def start():
        total_ref[...] = before_ref[...] if started else jnp.zeros_like(total_ref)

    block = mine_ref.shape[1]
    here = pl.ds(pl.multiple_of((step + offset) * block, lane), block)
    total_ref[...] += jnp.dot(
        jnp.concatenate([mine_ref[...], theirs_ref[...]], axis=0),
        weight_ref[here],
        preferred_element_type=jnp.float32,
    )

    if finished:

        @pl.when(step == pl.num_programs(0) - 1)
        def finish():
            me = lax.axis_index("ctx")
            pairs = ordered_ref.shape[0] // 2
            for other in range(2):
                side = lax.bitwise_xor(lax.rem(me, 2), other)
                for distance in range(pairs):
                    pair = lax.bitwise_xor(lax.div(me, 2), distance)
                    begin = (other * pairs + distance) * rows_local
                    ordered_ref[2 * pair + side] = total_ref[begin : begin + rows_local]
            give_half(ordered_ref[...].reshape(total_ref.shape), keep_ref, give_ref, bit)


def down(mine, theirs, w_down, before, block, begin, finished, rows_local, bit):
    half, depth = mine.shape
    rows, columns = 2 * half, w_down.shape[1]
    operands = [mine, theirs, w_down]
    in_specs = [pl.BlockSpec((half, block), lambda j: (0, j))] * 2
    in_specs.append(pl.BlockSpec(memory_space=pltpu.VMEM))
    if before is not None:
        operands.append(before)
        in_specs.append(pl.BlockSpec((rows, columns), lambda j: (0, 0)))
    if finished:
        out = halves(rows, columns, bit)
        scratch = [
            pltpu.VMEM((rows, columns), jnp.float32),
            pltpu.VMEM((rows // rows_local, rows_local, columns), jnp.float32),
        ]
    else:
        out = [jax.ShapeDtypeStruct((rows, columns), jnp.float32)]
        scratch = []
    return pl.pallas_call(
        functools.partial(
            down_kernel,
            offset=begin,
            started=before is not None,
            finished=finished,
            rows_local=rows_local,
            bit=bit,
        ),
        grid=(depth // block,),
        in_specs=in_specs,
        out_specs=[pl.BlockSpec(part.shape, lambda j: (0, 0)) for part in out],
        out_shape=out,
        scratch_shapes=scratch,
        compiler_params=pltpu.CompilerParams(
            dimension_semantics=("arbitrary",), vmem_limit_bytes=small_vmem
        ),
        cost_estimate=pl.CostEstimate(
            flops=2 * rows * depth * columns, bytes_accessed=2 * depth * columns, transcendentals=0
        ),
    )(*operands)


def add_kernel(mine_ref, theirs_ref, keep_ref, give_ref, *, bit):
    give_half(mine_ref[...] + theirs_ref[...].astype(jnp.float32), keep_ref, give_ref, bit)


def add_and_split(mine, theirs, bit):
    return pl.pallas_call(
        functools.partial(add_kernel, bit=bit),
        out_shape=halves(*mine.shape, bit),
        compiler_params=pltpu.CompilerParams(vmem_limit_bytes=small_vmem),
    )(mine, theirs)


def spread(copies):
    gathered = lax.all_to_all(copies, "ctx", split_axis=0, concat_axis=0)
    return gathered.reshape((-1,) + copies.shape[2:])


def swap(block, axis, size, bit):
    return lax.ppermute(block, axis, [(i, i ^ bit) for i in range(size)])


def sum_over_head(block, size):
    bit = 1
    while bit < size:
        if bit > 1:
            block = block.astype(jnp.bfloat16)
        block = block.astype(jnp.float32) + swap(block, "head", size, bit).astype(jnp.float32)
        bit *= 2
    return block


def scatter_over_head(keep, give, size):
    bit = size // 2
    while bit > 1:
        theirs = swap(give, "head", size, bit)
        bit //= 2
        keep, give = add_and_split(keep, theirs, bit)
    return keep + swap(give, "head", size, bit)


def local_step(sources, heads):
    def local(
        queries, keys, values, offsets, lengths, residual, wo, norm_gain, w_gate, w_up, w_down
    ):
        head_size = keys.shape[2]
        kv_local = keys.shape[1]
        rows_local = queries.shape[0]
        groups = queries.shape[1] // (kv_local * head_size)
        batch = lengths.shape[0]
        width = residual.shape[1] * sources
        pair = jnp.concatenate([queries, swap(queries, "ctx", sources, 1)], axis=0)
        pieces = [pair] + [swap(pair, "ctx", sources, 2 * d) for d in range(1, sources // 2)]
        parts, w_gate, w_up, w_down = attention(
            pieces, lengths, offsets, keys, values, sources, groups, (w_gate, w_up, w_down)
        )
        parts = lax.all_to_all(parts, "ctx", split_axis=0, concat_axis=0)
        attended, copies = merge(parts, kv_local, groups)
        projected = jnp.dot(spread(copies), wo, preferred_element_type=jnp.float32)
        mixed = sum_over_head(projected, heads)
        units = w_gate.shape[1]
        block = math.gcd(units, 640)
        blocks = units // block
        cuts = sorted({0, blocks} | {blocks * part // 100 for part in (50,)})
        counts = tuple(end - begin for begin, end in zip(cuts, cuts[1:]))
        chunks = []
        for begin, end in zip(cuts, cuts[1:]):
            outs = gate_and_up(
                mixed, residual, norm_gain, w_gate, w_up, block, begin, end, sources
            )
            if begin == 0:
                stream = outs[0]
            chunks.append(outs[-2:])
        terms = []
        for keep, give in chunks:
            sums = pair_sums(keep, swap(give, "ctx", sources, 1))
            terms.append(
                [sums[0]] + [swap(sums[d], "ctx", sources, 2 * d) for d in range(1, len(sums))]
            )
        total = None
        for parts, begin, end in zip(terms, cuts, cuts[1:]):
            own = hidden_units(parts, block, width)
            mine = jnp.concatenate(
                [own] + [swap(own, "ctx", sources, 2 * d) for d in range(1, sources // 2)], axis=0
            )
            theirs = swap(mine, "ctx", sources, 1)
            total = down(
                mine, theirs, w_down, total, block, begin, end == blocks, rows_local, heads // 2
            )
            if end < blocks:
                (total,) = total
        ffn_out = scatter_over_head(*total, heads)
        return (attended, stream, ffn_out.astype(jnp.bfloat16))

    return local


def solution(mesh):
    return jax.shard_map(
        local_step(mesh.shape["ctx"], mesh.shape["head"]),
        mesh=mesh,
        in_specs=(
            P("ctx", "head"),
            P("ctx", "head", None),
            P("ctx", "head", None),
            P("ctx"),
            P(),
            P(None, "ctx"),
            P("head", "ctx"),
            P("ctx"),
            P("ctx", "head"),
            P("ctx", "head"),
            P("head", "ctx"),
        ),
        out_specs=(P("ctx", "head"), P(None, "ctx"), P("head", "ctx")),
        check_vma=False,
    )
```

```python
import functools
import math

import jax
import jax.numpy as jnp
from jax import lax
from jax.experimental import pallas as pl
from jax.experimental.pallas import tpu as pltpu
from jax.sharding import PartitionSpec as P

hidden_score = -1e30
lowest_base = -65536.0
largest_sum = 2.0**115
epsilon = 1e-06
lane = 128
stat_rows = 16
attention_vmem = 32 * 2**20
most_vmem = 56 * 2**20
small_vmem = 8 * 2**20


def split_heads(block, kv_local, head_size):
    flat = block.reshape(block.shape[0], kv_local * head_size)
    return [flat[:, h * head_size : (h + 1) * head_size] for h in range(kv_local)]


def hidden_slots(first_slot, count, limits):
    slot = lax.broadcasted_iota(jnp.int32, (count, limits.shape[1]), 0) + first_slot
    return jnp.where(slot < limits, 0.0, 1.0).astype(jnp.bfloat16)


def scores_of(key_block, hidden, query_cols):
    return jnp.dot(
        jnp.concatenate([key_block, hidden], axis=1), query_cols, preferred_element_type=jnp.float32
    )


def weighted_values(value_block, weights):
    return lax.dot_general(
        value_block,
        weights.astype(jnp.bfloat16),
        (((0,), (0,)), ((), ())),
        preferred_element_type=jnp.float32,
    )


def sublane_sums(weights):
    return jnp.sum(weights.reshape(weights.shape[0] // 8, 8, weights.shape[1]), axis=0)


def attention_kernel(
    *refs,
    pieces,
    kv_local,
    groups,
    sources,
    factor,
    carried,
):
    piece_refs, rest = refs[:pieces], refs[pieces:]
    probe_ref, length_ref, offset_ref, key_ref, value_ref, all_keys, all_values, *rest = rest
    weights_in, rest = rest[:carried], rest[carried:]
    out_ref, weights_out, rest = rest[0], rest[1 : 1 + carried], rest[1 + carried :]
    (
    query_ref,
    query_cols,
    base_ref,
    acc_ref,
    total_ref,
    plain_cols,
    spare_keys,
    spare_values,
    copy_sems,
    weight_sems,
    ) = rest
    step = pl.program_id(0)
    head_size = key_ref.shape[2]
    block = key_ref.shape[0]
    columns = query_cols.shape[2]
    batch = columns // groups
    extra = query_cols.shape[1] - head_size
    spot = lax.broadcasted_iota(jnp.int32, (1, extra), 1)
    ends = jnp.concatenate(
        [length_ref[...] - offset_ref[0], jnp.zeros((1, extra - batch), jnp.int32)], axis=1
    )
    limits = jnp.where(spot < batch, ends, jnp.where(spot == batch, -1, jnp.iinfo(jnp.int32).max))
    steps = all_keys.shape[0] // block

    turns = [
        max(t for t in range(1, steps + 1) if weight.shape[0] % (16 * t) == 0)
        for weight in weights_in
    ]

    def weight_copies(index, turn):
        rows = weights_in[index].shape[0] // turns[index]
        here = pl.ds(pl.multiple_of(turn * rows, 16), rows)
        return pltpu.make_async_copy(
            weights_in[index].at[here], weights_out[index].at[here], weight_sems.at[index, turn]
        )

    for index in range(carried):
        pl.when(step < turns[index])(weight_copies(index, step).start)

    @pl.when(step == 0)
    def start():
        me = lax.axis_index("ctx")
        upper = lax.rem(me, 2) == 1
        pair_rows = piece_refs[0].shape[0]
        half = pair_rows // 2
        for distance, piece_ref in enumerate(piece_refs):
            piece = piece_ref[...].astype(jnp.float32)
            low = jnp.where(upper, piece[half:], piece[:half])
            high = jnp.where(upper, piece[:half], piece[half:])
            place = pl.multiple_of(lax.bitwise_xor(lax.div(me, 2), distance) * pair_rows, pair_rows)
            query_ref[pl.ds(place, pair_rows)] = jnp.concatenate([low, high], axis=0)
        row = lax.broadcasted_iota(jnp.int32, (extra, columns), 0)
        column = lax.broadcasted_iota(jnp.int32, (extra, columns), 1)
        mask_rows = jnp.where(lax.rem(column, batch) == row, hidden_score, 0.0)
        hidden = hidden_slots(0, probe_ref.shape[0], limits)
        keys = split_heads(probe_ref[...], kv_local, head_size)
        for h in range(kv_local):
            rows = [
                query_ref[:, (h * groups + g) * head_size : (h * groups + g + 1) * head_size]
                for g in range(groups)
            ]
            turned = jnp.concatenate(rows, axis=0).T
            query_cols[h, :head_size] = turned.astype(jnp.bfloat16)
            query_cols[h, head_size:] = mask_rows.astype(jnp.bfloat16)
            top = jnp.max(scores_of(keys[h], hidden, query_cols[h]), axis=0, keepdims=True)
            base = jnp.maximum(top, lowest_base).astype(jnp.bfloat16).astype(jnp.float32)
            base_ref[h] = base
            query_cols[h, head_size:] = jnp.where(row == batch, -base, mask_rows).astype(jnp.bfloat16)
        acc_ref[...] = jnp.zeros_like(acc_ref)
        total_ref[...] = jnp.zeros_like(total_ref)

    hidden = hidden_slots(step * block, block, limits)
    keys = split_heads(key_ref[...], kv_local, head_size)
    values = split_heads(value_ref[...], kv_local, head_size)
    for h in range(kv_local):
        weights = jnp.exp2(scores_of(keys[h], hidden, query_cols[h]) * factor)
        total_ref[h] += sublane_sums(weights)
        acc_ref[h] += weighted_values(values[h], weights)

    @pl.when(step == pl.num_programs(0) - 1)
    def finish():
        @pl.when(jnp.logical_not(jnp.max(total_ref[...]) <= largest_sum))
        def redo():
            piece = spare_keys.shape[0]
            row = lax.broadcasted_iota(jnp.int32, (head_size + extra, columns), 0)
            for h in range(kv_local):
                old = query_cols[h].astype(jnp.float32)
                plain_cols[h] = jnp.where(row == head_size + batch, 0.0, old).astype(jnp.bfloat16)
            base_ref[...] = jnp.full_like(base_ref, lowest_base)
            acc_ref[...] = jnp.zeros_like(acc_ref)
            total_ref[...] = jnp.zeros_like(total_ref)

            def visit(turn, carry):
                first = turn * piece
                here = pl.ds(first, piece)
                get_keys = pltpu.make_async_copy(all_keys.at[here], spare_keys, copy_sems.at[0])
                get_values = pltpu.make_async_copy(
                    all_values.at[here], spare_values, copy_sems.at[1]
                )
                get_keys.start()
                get_values.start()
                get_keys.wait()
                get_values.wait()
                hidden = hidden_slots(first, piece, limits)
                keys = split_heads(spare_keys[...], kv_local, head_size)
                values = split_heads(spare_values[...], kv_local, head_size)
                for h in range(kv_local):
                    scores = scores_of(keys[h], hidden, plain_cols[h])
                    old = base_ref[h]
                    new = jnp.maximum(old, jnp.max(scores, axis=0, keepdims=True))
                    rescale = jnp.exp2((old - new) * factor)
                    weights = jnp.exp2((scores - new) * factor)
                    base_ref[h] = new
                    total_ref[h] = total_ref[h] * rescale + sublane_sums(weights)
                    acc_ref[h] = acc_ref[h] * rescale + weighted_values(values[h], weights)
                return carry

            lax.fori_loop(0, all_keys.shape[0] // piece, visit, 0)

        for index in range(carried):
            for turn in range(turns[index]):
                weight_copies(index, turn).wait()
        rows_local = batch // sources
        rows = groups * rows_local
        stats = jnp.zeros((stat_rows, columns), jnp.float32)
        stat_row = lax.broadcasted_iota(jnp.int32, (stat_rows, columns), 0)
        for h in range(kv_local):
            total = jnp.sum(total_ref[h], axis=0, keepdims=True)
            seen = total > 0.0
            safe = jnp.where(seen, total, 1.0)
            height = jnp.where(seen, base_ref[h] * factor + jnp.log2(safe), hidden_score)
            for piece in range(3):
                part = height.astype(jnp.bfloat16).astype(jnp.float32)
                stats = jnp.where(stat_row == 3 * h + piece, part, stats)
                height = height - part
            mean = (acc_ref[h] * (1.0 / safe)).T.astype(jnp.bfloat16)
            for c in range(sources):
                for g in range(groups):
                    out_ref[c, h * rows + g * rows_local : h * rows + (g + 1) * rows_local] = mean[
                        g * batch + c * rows_local : g * batch + (c + 1) * rows_local
                    ]
        here = lax.broadcasted_iota(jnp.int32, (columns, columns), 0)
        there = lax.broadcasted_iota(jnp.int32, (columns, columns), 1)
        source, place = lax.div(there, rows), lax.rem(there, rows)
        origin = lax.div(place, rows_local) * batch + source * rows_local + lax.rem(place, rows_local)
        stats = jnp.dot(
            stats.astype(jnp.bfloat16),
            jnp.where(here == origin, 1.0, 0.0).astype(jnp.bfloat16),
            preferred_element_type=jnp.float32,
        )
        for c in range(sources):
            out_ref[c, kv_local * rows :, :rows] = stats[:, c * rows : (c + 1) * rows].astype(
                jnp.bfloat16
            )


def attention(pieces, lengths, offsets, keys, values, sources, groups, weights=()):
    span, kv_local, head_size = keys.shape
    batch = len(pieces) * pieces[0].shape[0]
    columns = batch * groups
    block = math.gcd(4096, span)
    piece = math.gcd(1024, span)
    extra = -(-(batch + 1) // lane) * lane
    whole = lambda *shape: pl.BlockSpec(shape, lambda j: (0,) * len(shape))
    part = pl.BlockSpec((block, kv_local, head_size), lambda j: (j, 0, 0))
    out = (sources, kv_local * columns // sources + stat_rows, head_size)
    depth = head_size + extra
    probe = math.gcd(512, span)
    return pl.pallas_call(
        functools.partial(
            attention_kernel,
            pieces=len(pieces),
            kv_local=kv_local,
            groups=groups,
            sources=sources,
            factor=math.log2(math.e) / math.sqrt(head_size),
            carried=len(weights),
        ),
        grid=(span // block,),
        in_specs=[
            *[whole(*piece.shape) for piece in pieces],
            whole(probe, kv_local, head_size),
            whole(1, batch),
            pl.BlockSpec(memory_space=pltpu.SMEM),
            part,
            part,
            pl.BlockSpec(memory_space=pl.ANY),
            pl.BlockSpec(memory_space=pl.ANY),
        ]
        + [pl.BlockSpec(memory_space=pl.ANY)] * len(weights),
        out_specs=[whole(*out)] + [pl.BlockSpec(memory_space=pltpu.VMEM)] * len(weights),
        out_shape=[jax.ShapeDtypeStruct(out, jnp.bfloat16)]
        + [pltpu.VMEM(weight.shape, weight.dtype) for weight in weights],
        scratch_shapes=[
            pltpu.VMEM((batch, pieces[0].shape[1]), jnp.float32),
            pltpu.VMEM((kv_local, depth, columns), jnp.bfloat16),
            pltpu.VMEM((kv_local, 1, columns), jnp.float32),
            pltpu.VMEM((kv_local, head_size, columns), jnp.float32),
            pltpu.VMEM((kv_local, 8, columns), jnp.float32),
            pltpu.VMEM((kv_local, head_size + extra, columns), jnp.bfloat16),
            pltpu.VMEM((piece, kv_local, head_size), jnp.bfloat16),
            pltpu.VMEM((piece, kv_local, head_size), jnp.bfloat16),
            pltpu.SemaphoreType.DMA((2,)),
            pltpu.SemaphoreType.DMA((len(weights), span // block)),
        ],
        compiler_params=pltpu.CompilerParams(
            dimension_semantics=("arbitrary",), vmem_limit_bytes=attention_vmem
        ),
        cost_estimate=pl.CostEstimate(
            flops=4 * span * columns * kv_local * head_size,
            bytes_accessed=4 * span * kv_local * head_size,
            transcendentals=span * columns * kv_local,
        ),
    )(*pieces, keys, lengths[None], offsets, keys, values, keys, values, *weights)


def merge_kernel(part_ref, out_ref, copies_ref, *, kv_local, groups):
    sources, depth, head_size = part_ref.shape
    rows = (depth - stat_rows) // kv_local
    rows_local = rows // groups
    stats = part_ref[:, kv_local * rows :].astype(jnp.float32)
    stats = stats.reshape(sources * stat_rows, head_size).T
    for h in range(kv_local):
        heights = []
        for c in range(sources):
            first = c * stat_rows + 3 * h
            heights.append(
                stats[:rows, first : first + 1]
                + stats[:rows, first + 1 : first + 2]
                + stats[:rows, first + 2 : first + 3]
            )
        top = functools.reduce(jnp.maximum, heights)
        shares = [jnp.exp2(height - top) for height in heights]
        whole = sum(shares)
        mean = (
            sum(
                share * part_ref[c, h * rows : (h + 1) * rows].astype(jnp.float32)
                for c, share in enumerate(shares)
            )
            / whole
        )
        for g in range(groups):
            out_ref[:, (h * groups + g) * head_size : (h * groups + g + 1) * head_size] = mean[
                g * rows_local : (g + 1) * rows_local
            ].astype(jnp.bfloat16)
    copies_ref[...] = jnp.broadcast_to(out_ref[...][None], copies_ref.shape)


def merge(parts, kv_local, groups):
    sources, depth, head_size = parts.shape
    rows_local = (depth - stat_rows) // kv_local // groups
    width = kv_local * groups * head_size
    return pl.pallas_call(
        functools.partial(merge_kernel, kv_local=kv_local, groups=groups),
        out_specs=[pl.BlockSpec(memory_space=pltpu.VMEM)] * 2,
        out_shape=[
            pltpu.VMEM((rows_local, width), jnp.bfloat16),
            jax.ShapeDtypeStruct((sources, rows_local, width), jnp.bfloat16),
        ],
        compiler_params=pltpu.CompilerParams(vmem_limit_bytes=small_vmem),
    )(parts)


def terms_kernel(
    mixed_ref, residual_ref, gain_ref, gate_ref, up_ref, *rest, first, block, offset, sources
):
    if first:
        stream_ref, rest = rest[0], rest[1:]
    keep_ref, give_ref, normed = rest
    step = pl.program_id(0)
    upper = lax.rem(lax.axis_index("ctx"), 2) == 1
    rows_local = keep_ref.shape[1]

    def put(place, terms):
        for pair in range(sources // 2):
            begin = 2 * pair * rows_local
            low = terms[begin : begin + rows_local]
            high = terms[begin + rows_local : begin + 2 * rows_local]
            keep_ref[pair, :, place] = jnp.where(upper, high, low).astype(jnp.bfloat16)
            give_ref[pair, :, place] = jnp.where(upper, low, high).astype(jnp.bfloat16)

    @pl.when(step == 0)
    def start():
        combined = residual_ref[...].astype(jnp.float32) + mixed_ref[...]
        normed[...] = (combined * gain_ref[...]).astype(jnp.bfloat16)
        if first:
            stream_ref[...] = combined.astype(jnp.bfloat16)
        left = jnp.sum(combined * combined, axis=1, keepdims=True)
        spot = lax.broadcasted_iota(jnp.int32, (combined.shape[0], lane), 1)
        parts = jnp.zeros(spot.shape, jnp.float32)
        for piece in range(3):
            part = left.astype(jnp.bfloat16).astype(jnp.float32)
            parts = jnp.where(spot == piece, part, parts)
            left = left - part
        put(pl.ds(keep_ref.shape[2] - lane, lane), parts)

    begin = pl.multiple_of(step * 2 * block, lane)
    here = pl.ds(pl.multiple_of((step + offset) * block, lane), block)
    for place, weight_ref in ((begin, gate_ref), (begin + block, up_ref)):
        put(
            pl.ds(place, block),
            jnp.dot(normed[...], weight_ref[:, here], preferred_element_type=jnp.float32),
        )


def gate_and_up(mixed, residual, gain, w_gate, w_up, block, begin, end, sources):
    first = begin == 0
    rows, depth = residual.shape
    count = end - begin
    half = (sources // 2, rows // sources, 2 * block * count + lane)
    whole = lambda *shape: pl.BlockSpec(shape, lambda j: (0,) * len(shape))
    out_shape = [jax.ShapeDtypeStruct(half, jnp.bfloat16)] * 2
    out_specs = [whole(*half)] * 2
    if first:
        out_shape.insert(0, pltpu.VMEM((rows, depth), jnp.bfloat16))
        out_specs.insert(0, pl.BlockSpec(memory_space=pltpu.VMEM))
    return pl.pallas_call(
        functools.partial(
            terms_kernel, first=first, block=block, offset=begin, sources=sources
        ),
        grid=(count,),
        in_specs=[
            whole(rows, depth),
            whole(rows, depth),
            whole(1, depth),
            pl.BlockSpec(memory_space=pltpu.VMEM),
            pl.BlockSpec(memory_space=pltpu.VMEM),
        ],
        out_specs=out_specs,
        out_shape=out_shape,
        scratch_shapes=[pltpu.VMEM((rows, depth), jnp.bfloat16)],
        compiler_params=pltpu.CompilerParams(
            dimension_semantics=("arbitrary",), vmem_limit_bytes=small_vmem
        ),
        cost_estimate=pl.CostEstimate(
            flops=4 * rows * depth * block * count,
            bytes_accessed=4 * depth * block * count,
            transcendentals=0,
        ),
    )(mixed, residual, gain[None], w_gate, w_up)


def pair_kernel(keep_ref, theirs_ref, *out_refs):
    mine = lax.div(lax.axis_index("ctx"), 2)
    for distance, out_ref in enumerate(out_refs):
        pair = lax.bitwise_xor(mine, distance)
        total = keep_ref[pair].astype(jnp.float32) + theirs_ref[pair].astype(jnp.float32)
        out_ref[...] = total.astype(jnp.bfloat16)


def pair_sums(keep, theirs):
    return pl.pallas_call(
        pair_kernel,
        out_shape=[jax.ShapeDtypeStruct(keep.shape[1:], jnp.bfloat16)] * keep.shape[0],
        compiler_params=pltpu.CompilerParams(vmem_limit_bytes=small_vmem),
    )(keep, theirs)


def hidden_kernel(*refs, block, width):
    out_ref = refs[-1]
    terms = sum(part[...].astype(jnp.float32) for part in refs[:-1])
    last = terms.shape[1] - lane
    square_total = terms[:, last : last + 1] + terms[:, last + 1 : last + 2]
    square_total = square_total + terms[:, last + 2 : last + 3]
    scale = lax.rsqrt(square_total / width + epsilon)
    for begin in range(0, last, 2 * block):
        gate = scale * terms[:, begin : begin + block]
        upward = scale * terms[:, begin + block : begin + 2 * block]
        hidden = gate / (1.0 + jnp.exp(-gate)) * upward
        out_ref[:, begin // 2 : begin // 2 + block] = hidden.astype(jnp.bfloat16)


def hidden_units(parts, block, width):
    shape = (parts[0].shape[0], (parts[0].shape[1] - lane) // 2)
    return pl.pallas_call(
        functools.partial(hidden_kernel, block=block, width=width),
        out_shape=jax.ShapeDtypeStruct(shape, jnp.bfloat16),
        compiler_params=pltpu.CompilerParams(vmem_limit_bytes=small_vmem),
    )(*parts)


def give_parts(total, keep_ref, give_refs):
    me = lax.axis_index("head")
    keep_ref[...] = total[me]
    for distance, give_ref in enumerate(give_refs, 1):
        give_ref[...] = total[lax.bitwise_xor(me, distance)].astype(give_ref.dtype)


def head_parts(rows, columns, size):
    return [
        jax.ShapeDtypeStruct((rows // size, columns), jnp.float32 if d < 2 else jnp.bfloat16)
        for d in range(size)
    ]


def down_kernel(mine_ref, theirs_ref, weight_ref, *refs, offset, started, finished, rows_local, size):
    if started:
        before_ref, refs = refs[0], refs[1:]
    if finished:
        keep_ref, *give_refs, total_ref, ordered_ref, split_ref = refs
    else:
        (total_ref,) = refs
    step = pl.program_id(0)

    @pl.when(step == 0)
    def start():
        total_ref[...] = before_ref[...] if started else jnp.zeros_like(total_ref)

    block = mine_ref.shape[1]
    here = pl.ds(pl.multiple_of((step + offset) * block, lane), block)
    total_ref[...] += jnp.dot(
        jnp.concatenate([mine_ref[...], theirs_ref[...]], axis=0),
        weight_ref[here],
        preferred_element_type=jnp.float32,
    )

    if finished:

        @pl.when(step == pl.num_programs(0) - 1)
        def finish():
            me = lax.axis_index("ctx")
            pairs = ordered_ref.shape[0] // 2
            for other in range(2):
                side = lax.bitwise_xor(lax.rem(me, 2), other)
                for distance in range(pairs):
                    pair = lax.bitwise_xor(lax.div(me, 2), distance)
                    begin = (other * pairs + distance) * rows_local
                    ordered_ref[2 * pair + side] = total_ref[begin : begin + rows_local]
            split_ref[...] = ordered_ref[...].reshape(split_ref.shape)
            give_parts(split_ref, keep_ref, give_refs)


def down(mine, theirs, w_down, before, block, begin, finished, rows_local, size):
    half, depth = mine.shape
    rows, columns = 2 * half, w_down.shape[1]
    operands = [mine, theirs, w_down]
    in_specs = [pl.BlockSpec((half, block), lambda j: (0, j))] * 2
    in_specs.append(pl.BlockSpec(memory_space=pltpu.VMEM))
    if before is not None:
        operands.append(before)
        in_specs.append(pl.BlockSpec((rows, columns), lambda j: (0, 0)))
    if finished:
        out = head_parts(rows, columns, size)
        scratch = [
            pltpu.VMEM((rows, columns), jnp.float32),
            pltpu.VMEM((rows // rows_local, rows_local, columns), jnp.float32),
            pltpu.VMEM((size, rows // size, columns), jnp.float32),
        ]
    else:
        out = [jax.ShapeDtypeStruct((rows, columns), jnp.float32)]
        scratch = []
    return pl.pallas_call(
        functools.partial(
            down_kernel,
            offset=begin,
            started=before is not None,
            finished=finished,
            rows_local=rows_local,
            size=size,
        ),
        grid=(depth // block,),
        in_specs=in_specs,
        out_specs=[pl.BlockSpec(part.shape, lambda j: (0, 0)) for part in out],
        out_shape=out,
        scratch_shapes=scratch,
        compiler_params=pltpu.CompilerParams(
            dimension_semantics=("arbitrary",), vmem_limit_bytes=small_vmem
        ),
        cost_estimate=pl.CostEstimate(
            flops=2 * rows * depth * columns, bytes_accessed=2 * depth * columns, transcendentals=0
        ),
    )(*operands)


def spread(copies):
    gathered = lax.all_to_all(copies, "ctx", split_axis=0, concat_axis=0)
    return gathered.reshape((-1,) + copies.shape[2:])


def swap(block, axis, size, bit):
    return lax.ppermute(block, axis, [(i, i ^ bit) for i in range(size)])


def sum_over_head(block, size):
    bit = 1
    while bit < size:
        if bit > 1:
            block = block.astype(jnp.bfloat16)
        block = block.astype(jnp.float32) + swap(block, "head", size, bit).astype(jnp.float32)
        bit *= 2
    return block


def scatter_over_head(keep, *gives, size):
    theirs = [swap(give, "head", size, d) for d, give in enumerate(gives, 1)]
    return keep + sum(part.astype(jnp.float32) for part in theirs)


def local_step(sources, heads):
    def local(
        queries, keys, values, offsets, lengths, residual, wo, norm_gain, w_gate, w_up, w_down
    ):
        head_size = keys.shape[2]
        kv_local = keys.shape[1]
        rows_local = queries.shape[0]
        groups = queries.shape[1] // (kv_local * head_size)
        batch = lengths.shape[0]
        width = residual.shape[1] * sources
        pair = jnp.concatenate([queries, swap(queries, "ctx", sources, 1)], axis=0)
        pieces = [pair] + [swap(pair, "ctx", sources, 2 * d) for d in range(1, sources // 2)]
        parts, w_gate, w_up, w_down = attention(
            pieces, lengths, offsets, keys, values, sources, groups, (w_gate, w_up, w_down)
        )
        parts = lax.all_to_all(parts, "ctx", split_axis=0, concat_axis=0)
        attended, copies = merge(parts, kv_local, groups)
        projected = jnp.dot(spread(copies), wo, preferred_element_type=jnp.float32)
        mixed = sum_over_head(projected, heads)
        units = w_gate.shape[1]
        block = math.gcd(units, 640)
        blocks = units // block
        cuts = sorted({0, blocks} | {blocks * part // 100 for part in (50,)})
        counts = tuple(end - begin for begin, end in zip(cuts, cuts[1:]))
        chunks = []
        for begin, end in zip(cuts, cuts[1:]):
            outs = gate_and_up(
                mixed, residual, norm_gain, w_gate, w_up, block, begin, end, sources
            )
            if begin == 0:
                stream = outs[0]
            chunks.append(outs[-2:])
        terms = []
        for keep, give in chunks:
            sums = pair_sums(keep, swap(give, "ctx", sources, 1))
            terms.append(
                [sums[0]] + [swap(sums[d], "ctx", sources, 2 * d) for d in range(1, len(sums))]
            )
        total = None
        for parts, begin, end in zip(terms, cuts, cuts[1:]):
            own = hidden_units(parts, block, width)
            mine = jnp.concatenate(
                [own] + [swap(own, "ctx", sources, 2 * d) for d in range(1, sources // 2)], axis=0
            )
            theirs = swap(mine, "ctx", sources, 1)
            total = down(
                mine, theirs, w_down, total, block, begin, end == blocks, rows_local, heads
            )
            if end < blocks:
                (total,) = total
        ffn_out = scatter_over_head(*total, size=heads)
        return (attended, stream, ffn_out.astype(jnp.bfloat16))

    return local


def solution(mesh):
    return jax.shard_map(
        local_step(mesh.shape["ctx"], mesh.shape["head"]),
        mesh=mesh,
        in_specs=(
            P("ctx", "head"),
            P("ctx", "head", None),
            P("ctx", "head", None),
            P("ctx"),
            P(),
            P(None, "ctx"),
            P("head", "ctx"),
            P("ctx"),
            P("ctx", "head"),
            P("ctx", "head"),
            P("head", "ctx"),
        ),
        out_specs=(P("ctx", "head"), P(None, "ctx"), P("head", "ctx")),
        check_vma=False,
    )
```
